32 devices in a mesh: dev: 32 (over z, y, x, core).
Axes of the slice: x: 2, y: 2, z: 4, core: 2. Of those that a mesh axis runs over, the one named last changes fastest.
Arguments:
- embeddings: bfloat16 [32768, 768], P('dev')
Outputs:
- keep_weight: float32 [32768], P('dev')
All inputs are finite; a program needn't handle non-finite values.
Results may differ from the reference program's by a relative error of at most 0.0044.
Values may be sent and summed in bfloat16 or wider, within the bound.
A program may use at most 64 MiB of HBM per device.

```python
import math
import jax
import jax.numpy as jnp
import numpy as np
from jax import lax

D = 768
TILE = 1024
ROUNDS = 4
ROWS = 32768
N_DEV = 32


def draw_embeddings(key, part):
    key = jax.random.fold_in(key, 11)
    key_centers = jax.random.fold_in(key, 0)
    key_pick = jax.random.fold_in(key, 1)
    key_noise = jax.random.fold_in(key, 2)
    key_tight = jax.random.fold_in(key, 4)
    key_block = jax.random.fold_in(key, 5)
    blocks = ROWS // TILE
    clusters = blocks // 2 ** ROUNDS
    row_index = jnp.arange(ROWS, dtype=jnp.int32)
    block_index = row_index // TILE
    cluster_index = block_index % clusters
    limit = TILE - 3 * TILE * block_index // (4 * blocks)
    local_pick = jax.random.randint(key_pick, (ROWS,), 0, limit)
    center_index = cluster_index * TILE + local_pick
    block_draw = jax.random.uniform(key_block, (blocks,), jnp.float32)
    block_loose = block_draw[block_index]
    spread = jax.random.uniform(key_tight, (ROWS,), jnp.float32)
    centers = jax.random.normal(key_centers, (clusters * TILE, D), jnp.float32)
    noise = jax.random.normal(key_noise, (ROWS, D), jnp.float32)
    looseness = (0.004 + 0.33 * block_loose ** 5) * jnp.exp(-2.0 * spread)
    closeness = 1.0 - looseness
    across = jnp.sqrt(looseness * (2.0 - looseness))
    values = closeness[:, None] * centers[center_index] + across[:, None] * noise
    return values.astype(jnp.bfloat16)


def setup_inputs(seed: int = 0) -> dict:
    seeds = jax.random.split(jax.random.key(seed), 2)
    embeddings = draw_embeddings(jax.random.fold_in(seeds[1], 71), 0)
    return {"embeddings": embeddings}


sharpness = 10.0

def normalize(values):
    widened = values.astype(jnp.float32)
    scaled = widened * lax.rsqrt(lax.optimization_barrier(jnp.mean(widened * widened, axis=1, keepdims=True)) + 1e-06) / math.sqrt(values.shape[1])
    return scaled.astype(jnp.bfloat16)

def kernel_tile(left, right):
    similarity = jnp.dot(left, right.T, preferred_element_type=jnp.float32)
    return jnp.exp(sharpness * (similarity - 1.0))

def self_sums(block):
    return lax.optimization_barrier(jnp.sum(kernel_tile(block, block), axis=1))

def pair_sums(pair):
    tile_values = kernel_tile(pair[0], pair[1])
    return (lax.optimization_barrier(jnp.sum(tile_values, axis=1)), lax.optimization_barrier(jnp.sum(tile_values, axis=0)))

def reference(embeddings):
    normed = normalize(embeddings)
    blocks = normed.reshape(N_DEV, TILE, normed.shape[1])
    density = lax.map(self_sums, blocks)
    levels = N_DEV.bit_length() - 1
    players = np.arange(N_DEV)
    for round_index in range(ROUNDS):
        stride = 1 << levels - 1 - round_index
        lower = jnp.asarray(players[players & stride == 0], dtype=jnp.int32)
        upper = lower + stride
        row_sums, column_sums = lax.map(pair_sums, (blocks[lower], blocks[upper]))
        density = density.at[lower].add(row_sums).at[upper].add(column_sums)
    weights = 1.0 / density
    total = jnp.sum(weights)
    return (weights * (N_DEV * TILE) / total).reshape(N_DEV * TILE)
```

```python
import functools
import math

import jax
import jax.numpy as jnp
from jax import lax
from jax.experimental import pallas as pl
from jax.experimental.pallas import tpu as pltpu
from jax.sharding import PartitionSpec as P

ROUNDS = 4
LANES = 128
sharpness = 10.0


def bit_of(me, stride):
    return (me // stride) % 2


def flipped(me, stride):
    return me + stride * (1 - 2 * bit_of(me, stride))


def partners(n, me):
    top = n // 2
    found = []
    for first, second, extra in ((top, top // 2, 0), (top // 4, top // 8, 1)):
        parity = bit_of(me, first) + bit_of(me, second)
        if extra:
            parity = parity + me % 2
        parity = parity % 2
        a, b = flipped(me, first), flipped(me, second)
        target = a + parity * (b - a)
        source = b + parity * (a - b)
        found.append((target, source))
    return found


def normalize(values):
    widened = values.astype(jnp.float32)
    scaled = (
        widened
        * lax.rsqrt(jnp.mean(widened * widened, axis=1, keepdims=True) + 1e-06)
        / math.sqrt(values.shape[1])
    )
    return scaled.astype(jnp.bfloat16)


def kernel(
    n,
    emb_ref,
    out_ref,
    raw,
    normed,
    held,
    acc,
    sums,
    back,
    part,
    parts,
    load_sem,
    send_sem,
    recv_sem,
    sums_send,
    sums_recv,
    part_send,
    part_recv,
):
    rows = normed.shape[0]
    chunks = rows // LANES
    me = lax.axis_index("dev")

    def piece(c):
        return pl.ds(pl.multiple_of(c * LANES, LANES), LANES)

    def load(c):
        return pltpu.make_async_copy(
            emb_ref.at[piece(c)], raw.at[piece(c)], load_sem.at[c]
        )

    for c in range(chunks):
        load(c).start()

    barrier = pltpu.get_barrier_semaphore()

    @pl.loop(1, n)
    def _(step):
        pl.semaphore_signal(
            barrier,
            inc=1,
            device_id=((me + step) % n,),
            device_id_type=pl.DeviceIdType.MESH,
        )

    routes = partners(n, me)
    acc[...] = jnp.zeros_like(acc)

    def block_copy(way, c):
        return pltpu.make_async_remote_copy(
            src_ref=normed.at[piece(c)],
            dst_ref=held.at[way, piece(c)],
            send_sem=send_sem.at[way, c],
            recv_sem=recv_sem.at[way, c],
            device_id=(routes[way][0],),
            device_id_type=pl.DeviceIdType.MESH,
        )

    def sums_copy(way):
        return pltpu.make_async_remote_copy(
            src_ref=sums.at[way],
            dst_ref=back.at[way],
            send_sem=sums_send.at[way],
            recv_sem=sums_recv.at[way],
            device_id=(routes[way][1],),
            device_id_type=pl.DeviceIdType.MESH,
        )

    def prepare(c):
        load(c).wait()
        normed[piece(c), :] = normalize(raw[piece(c), :])

    prepare(0)
    pl.semaphore_wait(barrier, n - 1)
    for way in range(2):
        block_copy(way, 0).start()

    @pl.loop(1, chunks)
    def _(c):
        prepare(c)
        for way in range(2):
            block_copy(way, c).start()

    def tile(block):
        similarity = lax.dot_general(
            block,
            normed[...],
            (((1,), (1,)), ((), ())),
            preferred_element_type=jnp.float32,
        )
        values = jnp.exp(sharpness * (similarity - 1.0))
        acc[...] += jnp.sum(values.reshape(LANES // 8, 8, rows), axis=0)
        return values

    @pl.loop(0, chunks)
    def _(c):
        tile(normed[piece(c), :])

    for way in (1, 0):

        @pl.loop(0, chunks)
        def _(c):
            block_copy(way, c).wait_recv()
            values = tile(held[way, piece(c), :])
            folded = values[:, :LANES]
            for t in range(1, chunks):
                folded = folded + values[:, t * LANES : (t + 1) * LANES]
            sums[way, pl.ds(c, 1), :] = jnp.sum(folded.T, axis=0, keepdims=True)

        sums_copy(way).start()

    own = jnp.concatenate(
        [
            jnp.sum(acc[:, t * LANES : (t + 1) * LANES], axis=0, keepdims=True)
            for t in range(chunks)
        ],
        axis=0,
    )
    for way in (1, 0):
        sums_copy(way).wait_recv()
    weights = 1.0 / (own + back[0] + back[1])
    part[...] = jnp.sum(weights, axis=0, keepdims=True)

    @pl.loop(1, n)
    def _(step):
        pltpu.make_async_remote_copy(
            src_ref=part,
            dst_ref=parts.at[step - 1],
            send_sem=part_send,
            recv_sem=part_recv,
            device_id=((me + step) % n,),
            device_id_type=pl.DeviceIdType.MESH,
        ).start()

    for way in range(2):
        sums_copy(way).wait_send()

        @pl.loop(0, chunks)
        def _(c):
            block_copy(way, c).wait_send()

    pltpu.make_async_copy(parts, parts, part_recv).wait()
    total = jnp.sum(jnp.sum(parts[...], axis=0) + part[...])
    out_ref[...] = weights * (n * rows) / total
    pltpu.make_async_copy(parts, parts, part_send).wait()


def shards(embeddings):
    n = lax.axis_size("dev")
    rows, width = embeddings.shape
    chunks = rows // LANES
    tiles = ROUNDS // 2 + 1
    out = pl.pallas_call(
        functools.partial(kernel, n),
        out_shape=jax.ShapeDtypeStruct((chunks, LANES), jnp.float32),
        in_specs=[pl.BlockSpec(memory_space=pl.ANY)],
        out_specs=pl.BlockSpec(memory_space=pltpu.VMEM),
        scratch_shapes=[
            pltpu.VMEM((rows, width), jnp.bfloat16),
            pltpu.VMEM((rows, width), jnp.bfloat16),
            pltpu.VMEM((2, rows, width), jnp.bfloat16),
            pltpu.VMEM((8, rows), jnp.float32),
            pltpu.VMEM((2, chunks, LANES), jnp.float32),
            pltpu.VMEM((2, chunks, LANES), jnp.float32),
            pltpu.VMEM((1, LANES), jnp.float32),
            pltpu.VMEM((n - 1, 1, LANES), jnp.float32),
            pltpu.SemaphoreType.DMA((chunks,)),
            pltpu.SemaphoreType.DMA((2, chunks)),
            pltpu.SemaphoreType.DMA((2, chunks)),
            pltpu.SemaphoreType.DMA((2,)),
            pltpu.SemaphoreType.DMA((2,)),
            pltpu.SemaphoreType.DMA,
            pltpu.SemaphoreType.DMA,
        ],
        compiler_params=pltpu.CompilerParams(
            collective_id=0, has_side_effects=True, vmem_limit_bytes=63 * 2**20
        ),
        cost_estimate=pl.CostEstimate(
            flops=2 * tiles * rows * rows * width,
            bytes_accessed=2 * rows * width,
            transcendentals=tiles * rows * rows,
        ),
        name="pair_sums",
    )(embeddings)
    return out.reshape(rows)


def solution(mesh):
    return jax.shard_map(
        shards,
        mesh=mesh,
        in_specs=(P("dev", None),),
        out_specs=P("dev"),
        check_vma=False,
    )
```

```python
import functools
import math

import jax
import jax.numpy as jnp
from jax import lax
from jax.experimental import pallas as pl
from jax.experimental.pallas import tpu as pltpu
from jax.sharding import PartitionSpec as P

ROUNDS = 4
LANES = 128
DEPTH = (2, 4)
sharpness = 10.0


def bit_of(me, stride):
    return (me // stride) % 2


def flipped(me, stride):
    return me + stride * (1 - 2 * bit_of(me, stride))


def partners(n, me):
    top = n // 2
    found = []
    for first, second, extra in ((top, top // 2, 0), (top // 4, top // 8, 1)):
        parity = bit_of(me, first) + bit_of(me, second)
        if extra:
            parity = parity + me % 2
        parity = parity % 2
        a, b = flipped(me, first), flipped(me, second)
        target = a + parity * (b - a)
        source = b + parity * (a - b)
        found.append((target, source))
    return found


def normalize(values):
    widened = values.astype(jnp.float32)
    scaled = (
        widened
        * lax.rsqrt(jnp.mean(widened * widened, axis=1, keepdims=True) + 1e-06)
        / math.sqrt(values.shape[1])
    )
    return scaled.astype(jnp.bfloat16)


def kernel(
    n,
    emb_ref,
    out_ref,
    raw,
    normed,
    held,
    acc,
    sums,
    back,
    part,
    parts,
    load_sem,
    send_sem,
    recv_sem,
    sums_send,
    sums_recv,
    part_send,
    part_recv,
):
    rows = normed.shape[0]
    chunks = rows // LANES
    me = lax.axis_index("dev")

    def piece(c):
        return pl.ds(pl.multiple_of(c * LANES, LANES), LANES)

    def load(c):
        return pltpu.make_async_copy(
            emb_ref.at[piece(c)], raw.at[piece(c)], load_sem.at[c]
        )

    for c in range(chunks):
        load(c).start()

    barrier = pltpu.get_barrier_semaphore()

    @pl.loop(1, n)
    def _(step):
        pl.semaphore_signal(
            barrier,
            inc=1,
            device_id=((me + step) % n,),
            device_id_type=pl.DeviceIdType.MESH,
        )

    routes = partners(n, me)
    acc[...] = jnp.zeros_like(acc)

    def block_copy(way, c):
        return pltpu.make_async_remote_copy(
            src_ref=normed.at[piece(c)],
            dst_ref=held.at[way, piece(c)],
            send_sem=send_sem.at[way, c],
            recv_sem=recv_sem.at[way, c],
            device_id=(routes[way][0],),
            device_id_type=pl.DeviceIdType.MESH,
        )

    def sums_copy(way):
        return pltpu.make_async_remote_copy(
            src_ref=sums.at[way],
            dst_ref=back.at[way],
            send_sem=sums_send.at[way],
            recv_sem=sums_recv.at[way],
            device_id=(routes[way][1],),
            device_id_type=pl.DeviceIdType.MESH,
        )

    def prepare(c):
        load(c).wait()
        normed[piece(c), :] = normalize(raw[piece(c), :])

    prepare(0)
    pl.semaphore_wait(barrier, n - 1)
    for c in range(chunks):
        if c:
            prepare(c)
        for way in range(2):
            if c < DEPTH[way]:
                block_copy(way, c).start()

    def tile(block):
        similarity = lax.dot_general(
            block,
            normed[...],
            (((1,), (1,)), ((), ())),
            preferred_element_type=jnp.float32,
        )
        values = jnp.exp(sharpness * (similarity - 1.0))
        acc[...] += jnp.sum(values.reshape(LANES // 8, 8, rows), axis=0)
        return values

    def meet(way, c):
        block_copy(way, c).wait_recv()
        block_copy(way, c).wait_send()

        @pl.when(c + DEPTH[way] < chunks)
        def _():
            block_copy(way, c + DEPTH[way]).start()

        values = tile(held[way, piece(c), :])
        folded = values[:, :LANES]
        for t in range(1, chunks):
            folded = folded + values[:, t * LANES : (t + 1) * LANES]
        sums[way, pl.ds(c, 1), :] = jnp.sum(folded.T, axis=0, keepdims=True)

    @pl.loop(0, chunks)
    def _(c):
        tile(normed[piece(c), :])
        meet(1, c)
        meet(0, c)

    for way in (1, 0):
        sums_copy(way).start()

    own = jnp.concatenate(
        [
            jnp.sum(acc[:, t * LANES : (t + 1) * LANES], axis=0, keepdims=True)
            for t in range(chunks)
        ],
        axis=0,
    )
    for way in (1, 0):
        sums_copy(way).wait_recv()
    weights = 1.0 / (own + back[0] + back[1])
    part[...] = jnp.sum(weights, axis=0, keepdims=True)

    @pl.loop(1, n)
    def _(step):
        pltpu.make_async_remote_copy(
            src_ref=part,
            dst_ref=parts.at[step - 1],
            send_sem=part_send,
            recv_sem=part_recv,
            device_id=((me + step) % n,),
            device_id_type=pl.DeviceIdType.MESH,
        ).start()

    for way in range(2):
        sums_copy(way).wait_send()

    pltpu.make_async_copy(parts, parts, part_recv).wait()
    total = jnp.sum(jnp.sum(parts[...], axis=0) + part[...])
    out_ref[...] = weights * (n * rows) / total
    pltpu.make_async_copy(parts, parts, part_send).wait()


def shards(embeddings):
    n = lax.axis_size("dev")
    rows, width = embeddings.shape
    chunks = rows // LANES
    tiles = ROUNDS // 2 + 1
    out = pl.pallas_call(
        functools.partial(kernel, n),
        out_shape=jax.ShapeDtypeStruct((chunks, LANES), jnp.float32),
        in_specs=[pl.BlockSpec(memory_space=pl.ANY)],
        out_specs=pl.BlockSpec(memory_space=pltpu.VMEM),
        scratch_shapes=[
            pltpu.VMEM((rows, width), jnp.bfloat16),
            pltpu.VMEM((rows, width), jnp.bfloat16),
            pltpu.VMEM((2, rows, width), jnp.bfloat16),
            pltpu.VMEM((8, rows), jnp.float32),
            pltpu.VMEM((2, chunks, LANES), jnp.float32),
            pltpu.VMEM((2, chunks, LANES), jnp.float32),
            pltpu.VMEM((1, LANES), jnp.float32),
            pltpu.VMEM((n - 1, 1, LANES), jnp.float32),
            pltpu.SemaphoreType.DMA((chunks,)),
            pltpu.SemaphoreType.DMA((2, chunks)),
            pltpu.SemaphoreType.DMA((2, chunks)),
            pltpu.SemaphoreType.DMA((2,)),
            pltpu.SemaphoreType.DMA((2,)),
            pltpu.SemaphoreType.DMA,
            pltpu.SemaphoreType.DMA,
        ],
        compiler_params=pltpu.CompilerParams(
            collective_id=0, has_side_effects=True, vmem_limit_bytes=63 * 2**20
        ),
        cost_estimate=pl.CostEstimate(
            flops=2 * tiles * rows * rows * width,
            bytes_accessed=2 * rows * width,
            transcendentals=tiles * rows * rows,
        ),
        name="pair_sums",
    )(embeddings)
    return out.reshape(rows)


def solution(mesh):
    return jax.shard_map(
        shards,
        mesh=mesh,
        in_specs=(P("dev", None),),
        out_specs=P("dev"),
        check_vma=False,
    )
```

```python
import functools
import math

import jax
import jax.numpy as jnp
from jax import lax
from jax.experimental import pallas as pl
from jax.experimental.pallas import tpu as pltpu
from jax.sharding import PartitionSpec as P

ROUNDS = 4
LANES = 128
DEPTH = (2, 3)
CHUNK = 256
sharpness = 10.0


def bit_of(me, stride):
    return (me // stride) % 2


def flipped(me, stride):
    return me + stride * (1 - 2 * bit_of(me, stride))


def partners(n, me):
    top = n // 2
    found = []
    for first, second, extra in ((top, top // 2, 0), (top // 4, top // 8, 1)):
        parity = bit_of(me, first) + bit_of(me, second)
        if extra:
            parity = parity + me % 2
        parity = parity % 2
        a, b = flipped(me, first), flipped(me, second)
        target = a + parity * (b - a)
        source = b + parity * (a - b)
        found.append((target, source))
    return found


def normalize(values):
    widened = values.astype(jnp.float32)
    scaled = (
        widened
        * lax.rsqrt(jnp.mean(widened * widened, axis=1, keepdims=True) + 1e-06)
        / math.sqrt(values.shape[1])
    )
    return scaled.astype(jnp.bfloat16)


def kernel(
    n,
    emb_ref,
    out_ref,
    raw,
    normed,
    turned,
    held,
    acc,
    sums,
    back,
    part,
    parts,
    load_sem,
    send_sem,
    recv_sem,
    sums_send,
    sums_recv,
    part_send,
    part_recv,
):
    rows = normed.shape[0]
    chunks = rows // CHUNK
    me = lax.axis_index("dev")

    def piece(c):
        return pl.ds(pl.multiple_of(c * CHUNK, CHUNK), CHUNK)

    def load(c):
        return pltpu.make_async_copy(
            emb_ref.at[piece(c)], raw.at[piece(c)], load_sem.at[c]
        )

    for c in range(chunks):
        load(c).start()

    barrier = pltpu.get_barrier_semaphore()

    @pl.loop(1, n)
    def _(step):
        pl.semaphore_signal(
            barrier,
            inc=1,
            device_id=((me + step) % n,),
            device_id_type=pl.DeviceIdType.MESH,
        )

    routes = partners(n, me)
    acc[...] = jnp.zeros_like(acc)

    def block_copy(way, c):
        return pltpu.make_async_remote_copy(
            src_ref=normed.at[piece(c)],
            dst_ref=held.at[way, piece(c)],
            send_sem=send_sem.at[way, c],
            recv_sem=recv_sem.at[way, c],
            device_id=(routes[way][0],),
            device_id_type=pl.DeviceIdType.MESH,
        )

    def sums_copy(way):
        return pltpu.make_async_remote_copy(
            src_ref=sums.at[way],
            dst_ref=back.at[way],
            send_sem=sums_send.at[way],
            recv_sem=sums_recv.at[way],
            device_id=(routes[way][1],),
            device_id_type=pl.DeviceIdType.MESH,
        )

    def prepare(c):
        load(c).wait()
        normed[piece(c), :] = normalize(raw[piece(c), :])

    def turn(c):
        turned[:, piece(c)] = normed[piece(c), :].T

    prepare(0)
    pl.semaphore_wait(barrier, n - 1)
    for c in range(chunks):
        if c:
            prepare(c)
        for way in range(2):
            if c < DEPTH[way]:
                block_copy(way, c).start()

    for c in range(chunks):
        turn(c)

    def tile(block, fold):
        folded = None
        for t in range(chunks):
            columns = slice(t * CHUNK, (t + 1) * CHUNK)
            similarity = jnp.dot(
                block, turned[:, columns], preferred_element_type=jnp.float32
            )
            values = jnp.exp(sharpness * (similarity - 1.0))
            acc[:, columns] += jnp.sum(
                values.reshape(CHUNK // 8, 8, CHUNK), axis=0
            )
            if fold:
                for u in range(0, CHUNK, LANES):
                    term = values[:, u : u + LANES]
                    folded = term if folded is None else folded + term
        return folded

    def meet(way, c):
        block_copy(way, c).wait_recv()
        block_copy(way, c).wait_send()

        @pl.when(c + DEPTH[way] < chunks)
        def _():
            block_copy(way, c + DEPTH[way]).start()

        folded = tile(held[way, piece(c), :], True)
        for u in range(CHUNK // LANES):
            turned_sums = folded[u * LANES : (u + 1) * LANES].T
            sums[way, pl.ds(c * (CHUNK // LANES) + u, 1), :] = jnp.sum(
                turned_sums, axis=0, keepdims=True
            )

    @pl.loop(0, chunks)
    def _(c):
        tile(normed[piece(c), :], False)
        meet(1, c)
        meet(0, c)

    for way in (1, 0):
        sums_copy(way).start()

    own = jnp.concatenate(
        [
            jnp.sum(acc[:, t * LANES : (t + 1) * LANES], axis=0, keepdims=True)
            for t in range(rows // LANES)
        ],
        axis=0,
    )
    for way in (1, 0):
        sums_copy(way).wait_recv()
    weights = 1.0 / (own + back[0] + back[1])
    part[...] = jnp.sum(weights, axis=0, keepdims=True)

    @pl.loop(1, n)
    def _(step):
        pltpu.make_async_remote_copy(
            src_ref=part,
            dst_ref=parts.at[step - 1],
            send_sem=part_send,
            recv_sem=part_recv,
            device_id=((me + step) % n,),
            device_id_type=pl.DeviceIdType.MESH,
        ).start()

    for way in range(2):
        sums_copy(way).wait_send()

    pltpu.make_async_copy(parts, parts, part_recv).wait()
    total = jnp.sum(jnp.sum(parts[...], axis=0) + part[...])
    out_ref[...] = weights * (n * rows) / total
    pltpu.make_async_copy(parts, parts, part_send).wait()


def shards(embeddings):
    n = lax.axis_size("dev")
    rows, width = embeddings.shape
    chunks = rows // CHUNK
    slabs = rows // LANES
    tiles = ROUNDS // 2 + 1
    out = pl.pallas_call(
        functools.partial(kernel, n),
        out_shape=jax.ShapeDtypeStruct((slabs, LANES), jnp.float32),
        in_specs=[pl.BlockSpec(memory_space=pl.ANY)],
        out_specs=pl.BlockSpec(memory_space=pltpu.VMEM),
        scratch_shapes=[
            pltpu.VMEM((rows, width), jnp.bfloat16),
            pltpu.VMEM((rows, width), jnp.bfloat16),
            pltpu.VMEM((width, rows), jnp.bfloat16),
            pltpu.VMEM((2, rows, width), jnp.bfloat16),
            pltpu.VMEM((8, rows), jnp.float32),
            pltpu.VMEM((2, slabs, LANES), jnp.float32),
            pltpu.VMEM((2, slabs, LANES), jnp.float32),
            pltpu.VMEM((1, LANES), jnp.float32),
            pltpu.VMEM((n - 1, 1, LANES), jnp.float32),
            pltpu.SemaphoreType.DMA((chunks,)),
            pltpu.SemaphoreType.DMA((2, chunks)),
            pltpu.SemaphoreType.DMA((2, chunks)),
            pltpu.SemaphoreType.DMA((2,)),
            pltpu.SemaphoreType.DMA((2,)),
            pltpu.SemaphoreType.DMA,
            pltpu.SemaphoreType.DMA,
        ],
        compiler_params=pltpu.CompilerParams(
            collective_id=0, has_side_effects=True, vmem_limit_bytes=63 * 2**20
        ),
        cost_estimate=pl.CostEstimate(
            flops=2 * tiles * rows * rows * width,
            bytes_accessed=2 * rows * width,
            transcendentals=tiles * rows * rows,
        ),
        name="pair_sums",
    )(embeddings)
    return out.reshape(rows)


def solution(mesh):
    return jax.shard_map(
        shards,
        mesh=mesh,
        in_specs=(P("dev", None),),
        out_specs=P("dev"),
        check_vma=False,
    )
```

```python
import functools
import math

import jax
import jax.numpy as jnp
from jax import lax
from jax.experimental import pallas as pl
from jax.experimental.pallas import tpu as pltpu
from jax.sharding import PartitionSpec as P

ROUNDS = 4
LANES = 128
DEPTH = (2, 3)
CHUNK = 256
sharpness = 10.0


def bit_of(me, stride):
    return (me // stride) % 2


def flipped(me, stride):
    return me + stride * (1 - 2 * bit_of(me, stride))


def partners(n, me):
    top = n // 2
    found = []
    for first, second, extra in ((top, top // 2, 0), (top // 4, top // 8, 1)):
        parity = bit_of(me, first) + bit_of(me, second)
        if extra:
            parity = parity + me % 2
        parity = parity % 2
        a, b = flipped(me, first), flipped(me, second)
        target = a + parity * (b - a)
        source = b + parity * (a - b)
        found.append((target, source))
    return found


def normalize(values):
    widened = values.astype(jnp.float32)
    scaled = (
        widened
        * lax.rsqrt(jnp.mean(widened * widened, axis=1, keepdims=True) + 1e-06)
        / math.sqrt(values.shape[1])
    )
    return scaled.astype(jnp.bfloat16)


def kernel(
    n,
    emb_ref,
    out_ref,
    raw,
    normed,
    turned,
    held,
    acc,
    sums,
    back,
    part,
    near_parts,
    far_parts,
    load_sem,
    send_sem,
    recv_sem,
    sums_send,
    sums_recv,
    part_send,
    part_recv,
):
    rows = normed.shape[0]
    chunks = rows // CHUNK
    me = lax.axis_index("dev")

    def piece(c):
        return pl.ds(pl.multiple_of(c * CHUNK, CHUNK), CHUNK)

    def load(c):
        return pltpu.make_async_copy(
            emb_ref.at[piece(c)], raw.at[piece(c)], load_sem.at[c]
        )

    near = n // 4
    groups = ((near, near_parts), (4, far_parts))

    def peer(peers, step):
        if peers == near:
            return me // near * near + (me % near + step) % near
        return (me + step * near) % n

    for c in range(chunks):
        load(c).start()

    barrier = pltpu.get_barrier_semaphore()

    for peers, _ in groups:

        @pl.loop(1, peers)
        def _(step):
            pl.semaphore_signal(
                barrier,
                inc=1,
                device_id=(peer(peers, step),),
                device_id_type=pl.DeviceIdType.MESH,
            )

    routes = partners(n, me)
    acc[...] = jnp.zeros_like(acc)

    def block_copy(way, c):
        return pltpu.make_async_remote_copy(
            src_ref=normed.at[piece(c)],
            dst_ref=held.at[way, piece(c)],
            send_sem=send_sem.at[way, c],
            recv_sem=recv_sem.at[way, c],
            device_id=(routes[way][0],),
            device_id_type=pl.DeviceIdType.MESH,
        )

    def sums_copy(way):
        return pltpu.make_async_remote_copy(
            src_ref=sums.at[way],
            dst_ref=back.at[way],
            send_sem=sums_send.at[way],
            recv_sem=sums_recv.at[way],
            device_id=(routes[way][1],),
            device_id_type=pl.DeviceIdType.MESH,
        )

    def prepare(c):
        load(c).wait()
        normed[piece(c), :] = normalize(raw[piece(c), :])

    def turn(c):
        turned[:, piece(c)] = normed[piece(c), :].T

    prepare(0)
    pl.semaphore_wait(barrier, near + 2)
    for c in range(chunks):
        if c:
            prepare(c)
        for way in range(2):
            if c < DEPTH[way]:
                block_copy(way, c).start()

    for c in range(chunks):
        turn(c)

    def tile(block, fold):
        folded = None
        for t in range(chunks):
            columns = slice(t * CHUNK, (t + 1) * CHUNK)
            similarity = jnp.dot(
                block, turned[:, columns], preferred_element_type=jnp.float32
            )
            values = jnp.exp(sharpness * (similarity - 1.0))
            acc[:, columns] += jnp.sum(
                values.reshape(CHUNK // 8, 8, CHUNK), axis=0
            )
            if fold:
                for u in range(0, CHUNK, LANES):
                    term = values[:, u : u + LANES]
                    folded = term if folded is None else folded + term
        return folded

    def meet(way, c):
        block_copy(way, c).wait_recv()
        block_copy(way, c).wait_send()

        @pl.when(c + DEPTH[way] < chunks)
        def _():
            block_copy(way, c + DEPTH[way]).start()

        folded = tile(held[way, piece(c), :], True)
        for u in range(CHUNK // LANES):
            turned_sums = folded[u * LANES : (u + 1) * LANES].T
            sums[way, pl.ds(c * (CHUNK // LANES) + u, 1), :] = jnp.sum(
                turned_sums, axis=0, keepdims=True
            )

    @pl.loop(0, chunks)
    def _(c):
        tile(normed[piece(c), :], False)
        meet(1, c)
        meet(0, c)

    for way in (1, 0):
        sums_copy(way).start()

    own = jnp.concatenate(
        [
            jnp.sum(acc[:, t * LANES : (t + 1) * LANES], axis=0, keepdims=True)
            for t in range(rows // LANES)
        ],
        axis=0,
    )
    for way in (1, 0):
        sums_copy(way).wait_recv()
    weights = 1.0 / (own + back[0] + back[1])
    part[0] = jnp.sum(weights, axis=0, keepdims=True)

    for stage, (peers, parts) in enumerate(groups):

        @pl.loop(1, peers)
        def _(step):
            pltpu.make_async_remote_copy(
                src_ref=part.at[stage],
                dst_ref=parts.at[step - 1],
                send_sem=part_send.at[stage],
                recv_sem=part_recv.at[stage],
                device_id=(peer(peers, step),),
                device_id_type=pl.DeviceIdType.MESH,
            ).start()

        if stage == 0:
            for way in range(2):
                sums_copy(way).wait_send()
        pltpu.make_async_copy(parts, parts, part_recv.at[stage]).wait()
        part[stage + 1] = part[stage] + jnp.sum(parts[...], axis=0)

    total = jnp.sum(part[2], axis=1, keepdims=True)
    out_ref[...] = weights * (n * rows) / total
    for stage, (peers, parts) in enumerate(groups):
        pltpu.make_async_copy(parts, parts, part_send.at[stage]).wait()


def shards(embeddings):
    n = lax.axis_size("dev")
    rows, width = embeddings.shape
    chunks = rows // CHUNK
    slabs = rows // LANES
    tiles = ROUNDS // 2 + 1
    out = pl.pallas_call(
        functools.partial(kernel, n),
        out_shape=jax.ShapeDtypeStruct((slabs, LANES), jnp.float32),
        in_specs=[pl.BlockSpec(memory_space=pl.ANY)],
        out_specs=pl.BlockSpec(memory_space=pltpu.VMEM),
        scratch_shapes=[
            pltpu.VMEM((rows, width), jnp.bfloat16),
            pltpu.VMEM((rows, width), jnp.bfloat16),
            pltpu.VMEM((width, rows), jnp.bfloat16),
            pltpu.VMEM((2, rows, width), jnp.bfloat16),
            pltpu.VMEM((8, rows), jnp.float32),
            pltpu.VMEM((2, slabs, LANES), jnp.float32),
            pltpu.VMEM((2, slabs, LANES), jnp.float32),
            pltpu.VMEM((3, 1, LANES), jnp.float32),
            pltpu.VMEM((n // 4 - 1, 1, LANES), jnp.float32),
            pltpu.VMEM((3, 1, LANES), jnp.float32),
            pltpu.SemaphoreType.DMA((chunks,)),
            pltpu.SemaphoreType.DMA((2, chunks)),
            pltpu.SemaphoreType.DMA((2, chunks)),
            pltpu.SemaphoreType.DMA((2,)),
            pltpu.SemaphoreType.DMA((2,)),
            pltpu.SemaphoreType.DMA((2,)),
            pltpu.SemaphoreType.DMA((2,)),
        ],
        compiler_params=pltpu.CompilerParams(
            collective_id=0, has_side_effects=True, vmem_limit_bytes=63 * 2**20
        ),
        cost_estimate=pl.CostEstimate(
            flops=2 * tiles * rows * rows * width,
            bytes_accessed=2 * rows * width,
            transcendentals=tiles * rows * rows,
        ),
        name="pair_sums",
    )(embeddings)
    return out.reshape(rows)


def solution(mesh):
    return jax.shard_map(
        shards,
        mesh=mesh,
        in_specs=(P("dev", None),),
        out_specs=P("dev"),
        check_vma=False,
    )
```

```python
import functools
import math

import jax
import jax.numpy as jnp
from jax import lax
from jax.experimental import pallas as pl
from jax.experimental.pallas import tpu as pltpu
from jax.sharding import PartitionSpec as P

ROUNDS = 4
LANES = 128
DEPTH = (4, 1)
CHUNK = 256
sharpness = 10.0


def bit_of(me, stride):
    return (me // stride) % 2


def flipped(me, stride):
    return me + stride * (1 - 2 * bit_of(me, stride))


def partners(n, me):
    top = n // 2
    found = []
    for first, second, extra in ((top, top // 2, 0), (top // 4, top // 8, 1)):
        parity = bit_of(me, first) + bit_of(me, second)
        if extra:
            parity = parity + me % 2
        parity = parity % 2
        a, b = flipped(me, first), flipped(me, second)
        target = a + parity * (b - a)
        source = b + parity * (a - b)
        found.append((target, source))
    return found


def normalize(values):
    widened = values.astype(jnp.float32)
    scaled = (
        widened
        * lax.rsqrt(jnp.mean(widened * widened, axis=1, keepdims=True) + 1e-06)
        / math.sqrt(values.shape[1])
    )
    return scaled.astype(jnp.bfloat16)


def kernel(
    n,
    emb_ref,
    out_ref,
    raw,
    normed,
    turned,
    held,
    acc,
    sums,
    back,
    part,
    parts,
    load_sem,
    send_sem,
    recv_sem,
    sums_send,
    sums_recv,
    part_send,
    part_recv,
):
    rows = normed.shape[0]
    chunks = rows // CHUNK
    me = lax.axis_index("dev")

    def piece(c):
        return pl.ds(pl.multiple_of(c * CHUNK, CHUNK), CHUNK)

    def load(c):
        return pltpu.make_async_copy(
            emb_ref.at[piece(c)], raw.at[piece(c)], load_sem.at[c]
        )

    for c in range(chunks):
        load(c).start()

    barrier = pltpu.get_barrier_semaphore()

    @pl.loop(1, n)
    def _(step):
        pl.semaphore_signal(
            barrier,
            inc=1,
            device_id=((me + step) % n,),
            device_id_type=pl.DeviceIdType.MESH,
        )

    routes = partners(n, me)
    acc[...] = jnp.zeros_like(acc)

    def block_copy(way, c):
        return pltpu.make_async_remote_copy(
            src_ref=normed.at[piece(c)],
            dst_ref=held.at[way, piece(c)],
            send_sem=send_sem.at[way, c],
            recv_sem=recv_sem.at[way, c],
            device_id=(routes[way][0],),
            device_id_type=pl.DeviceIdType.MESH,
        )

    def sums_copy(way):
        return pltpu.make_async_remote_copy(
            src_ref=sums.at[way],
            dst_ref=back.at[way],
            send_sem=sums_send.at[way],
            recv_sem=sums_recv.at[way],
            device_id=(routes[way][1],),
            device_id_type=pl.DeviceIdType.MESH,
        )

    def prepare(c):
        load(c).wait()
        normed[piece(c), :] = normalize(raw[piece(c), :])

    def turn(c):
        turned[:, piece(c)] = normed[piece(c), :].T

    prepare(0)
    pl.semaphore_wait(barrier, n - 1)
    for c in range(chunks):
        if c:
            prepare(c)
        for way in range(2):
            if c < DEPTH[way]:
                block_copy(way, c).start()

    for c in range(chunks):
        turn(c)

    def tile(block, fold):
        folded = None
        for t in range(chunks):
            columns = slice(t * CHUNK, (t + 1) * CHUNK)
            similarity = jnp.dot(
                block, turned[:, columns], preferred_element_type=jnp.float32
            )
            values = jnp.exp(sharpness * (similarity - 1.0))
            acc[:, columns] += jnp.sum(
                values.reshape(CHUNK // 8, 8, CHUNK), axis=0
            )
            if fold:
                for u in range(0, CHUNK, LANES):
                    term = values[:, u : u + LANES]
                    folded = term if folded is None else folded + term
        return folded

    def meet(way, c):
        block_copy(way, c).wait_recv()
        block_copy(way, c).wait_send()

        @pl.when(c + DEPTH[way] < chunks)
        def _():
            block_copy(way, c + DEPTH[way]).start()

        folded = tile(held[way, piece(c), :], True)
        for u in range(CHUNK // LANES):
            turned_sums = folded[u * LANES : (u + 1) * LANES].T
            sums[way, pl.ds(c * (CHUNK // LANES) + u, 1), :] = jnp.sum(
                turned_sums, axis=0, keepdims=True
            )

    @pl.loop(0, chunks)
    def _(c):
        tile(normed[piece(c), :], False)
        meet(1, c)
        meet(0, c)

    for way in (1, 0):
        sums_copy(way).start()

    own = jnp.concatenate(
        [
            jnp.sum(acc[:, t * LANES : (t + 1) * LANES], axis=0, keepdims=True)
            for t in range(rows // LANES)
        ],
        axis=0,
    )
    for way in (1, 0):
        sums_copy(way).wait_recv()
    weights = 1.0 / (own + back[0] + back[1])
    part[...] = jnp.sum(weights, axis=0, keepdims=True)

    @pl.loop(1, n)
    def _(step):
        pltpu.make_async_remote_copy(
            src_ref=part,
            dst_ref=parts.at[step - 1],
            send_sem=part_send,
            recv_sem=part_recv,
            device_id=((me + step) % n,),
            device_id_type=pl.DeviceIdType.MESH,
        ).start()

    for way in range(2):
        sums_copy(way).wait_send()

    pltpu.make_async_copy(parts, parts, part_recv).wait()
    total = jnp.sum(jnp.sum(parts[...], axis=0) + part[...])
    out_ref[...] = weights * (n * rows) / total
    pltpu.make_async_copy(parts, parts, part_send).wait()


def shards(embeddings):
    n = lax.axis_size("dev")
    rows, width = embeddings.shape
    chunks = rows // CHUNK
    slabs = rows // LANES
    tiles = ROUNDS // 2 + 1
    out = pl.pallas_call(
        functools.partial(kernel, n),
        out_shape=jax.ShapeDtypeStruct((slabs, LANES), jnp.float32),
        in_specs=[pl.BlockSpec(memory_space=pl.ANY)],
        out_specs=pl.BlockSpec(memory_space=pltpu.VMEM),
        scratch_shapes=[
            pltpu.VMEM((rows, width), jnp.bfloat16),
            pltpu.VMEM((rows, width), jnp.bfloat16),
            pltpu.VMEM((width, rows), jnp.bfloat16),
            pltpu.VMEM((2, rows, width), jnp.bfloat16),
            pltpu.VMEM((8, rows), jnp.float32),
            pltpu.VMEM((2, slabs, LANES), jnp.float32),
            pltpu.VMEM((2, slabs, LANES), jnp.float32),
            pltpu.VMEM((1, LANES), jnp.float32),
            pltpu.VMEM((n - 1, 1, LANES), jnp.float32),
            pltpu.SemaphoreType.DMA((chunks,)),
            pltpu.SemaphoreType.DMA((2, chunks)),
            pltpu.SemaphoreType.DMA((2, chunks)),
            pltpu.SemaphoreType.DMA((2,)),
            pltpu.SemaphoreType.DMA((2,)),
            pltpu.SemaphoreType.DMA,
            pltpu.SemaphoreType.DMA,
        ],
        compiler_params=pltpu.CompilerParams(
            collective_id=0, has_side_effects=True, vmem_limit_bytes=63 * 2**20
        ),
        cost_estimate=pl.CostEstimate(
            flops=2 * tiles * rows * rows * width,
            bytes_accessed=2 * rows * width,
            transcendentals=tiles * rows * rows,
        ),
        name="pair_sums",
    )(embeddings)
    return out.reshape(rows)


def solution(mesh):
    return jax.shard_map(
        shards,
        mesh=mesh,
        in_specs=(P("dev", None),),
        out_specs=P("dev"),
        check_vma=False,
    )
```

```python
import functools
import math

import jax
import jax.numpy as jnp
from jax import lax
from jax.experimental import pallas as pl
from jax.experimental.pallas import tpu as pltpu
from jax.sharding import PartitionSpec as P

ROUNDS = 4
LANES = 128
CHUNK = 256
sharpness = 10.0


def bit_of(me, stride):
    return (me // stride) % 2


def flipped(me, stride):
    return me + stride * (1 - 2 * bit_of(me, stride))


def partners(n, me):
    top = n // 2
    found = []
    for first, second, extra in ((top, top // 2, 0), (top // 4, top // 8, 1)):
        parity = bit_of(me, first) + bit_of(me, second)
        if extra:
            parity = parity + me % 2
        parity = parity % 2
        a, b = flipped(me, first), flipped(me, second)
        target = a + parity * (b - a)
        source = b + parity * (a - b)
        found.append((target, source))
    return found


def normalize(values):
    widened = values.astype(jnp.float32)
    scaled = (
        widened
        * lax.rsqrt(jnp.mean(widened * widened, axis=1, keepdims=True) + 1e-06)
        / math.sqrt(values.shape[1])
    )
    return scaled.astype(jnp.bfloat16)


def kernel(
    n,
    emb_ref,
    out_ref,
    raw,
    normed,
    turned,
    held,
    acc,
    sums,
    back,
    part,
    parts,
    load_sem,
    send_sem,
    recv_sem,
    sums_send,
    sums_recv,
    part_send,
    part_recv,
    known,
):
    rows = normed.shape[0]
    chunks = rows // CHUNK
    me = lax.axis_index("dev")

    def piece(c):
        return pl.ds(pl.multiple_of(c * CHUNK, CHUNK), CHUNK)

    def load(c):
        return pltpu.make_async_copy(
            emb_ref.at[piece(c)], raw.at[piece(c)], load_sem.at[c]
        )

    levels = n.bit_length() - 1
    flips = [flipped(me, 1 << level) - me for level in range(levels)]

    def across(mask):
        return me + sum(flips[level] for level in range(levels) if mask >> level & 1)

    barrier = pltpu.get_barrier_semaphore()
    for level in range(levels):
        pl.semaphore_signal(
            barrier,
            inc=1,
            device_id=(across(1 << level),),
            device_id_type=pl.DeviceIdType.MESH,
        )
    for c in range(chunks):
        load(c).start()

    routes = partners(n, me)
    acc[...] = jnp.zeros_like(acc)

    def block_copy(way, c):
        return pltpu.make_async_remote_copy(
            src_ref=normed.at[piece(c)],
            dst_ref=held.at[way, piece(c)],
            send_sem=send_sem.at[way, c],
            recv_sem=recv_sem.at[way, c],
            device_id=(routes[way][0],),
            device_id_type=pl.DeviceIdType.MESH,
        )

    def sums_copy(way):
        return pltpu.make_async_remote_copy(
            src_ref=sums.at[way],
            dst_ref=back.at[way],
            send_sem=sums_send.at[way],
            recv_sem=sums_recv.at[way],
            device_id=(routes[way][1],),
            device_id_type=pl.DeviceIdType.MESH,
        )

    def prepare(c):
        load(c).wait()
        normed[piece(c), :] = normalize(raw[piece(c), :])

    def turn(c):
        turned[:, piece(c)] = normed[piece(c), :].T

    prepare(0)
    pl.semaphore_wait(barrier, levels)
    for c in range(chunks):
        if c:
            prepare(c)
        for way in range(2):
            block_copy(way, c).start()

    for c in range(chunks):
        turn(c)

    def tile(block, fold):
        folded = None
        for t in range(chunks):
            columns = slice(t * CHUNK, (t + 1) * CHUNK)
            similarity = jnp.dot(
                block, turned[:, columns], preferred_element_type=jnp.float32
            )
            values = jnp.exp(sharpness * (similarity - 1.0))
            acc[:, columns] += jnp.sum(
                values.reshape(CHUNK // 8, 8, CHUNK), axis=0
            )
            if fold:
                for u in range(0, CHUNK, LANES):
                    term = values[:, u : u + LANES]
                    folded = term if folded is None else folded + term
        return folded

    def meet(way, c):
        block_copy(way, c).wait_recv()
        folded = tile(held[way, piece(c), :], True)
        for u in range(CHUNK // LANES):
            turned_sums = folded[u * LANES : (u + 1) * LANES].T
            sums[way, pl.ds(c * (CHUNK // LANES) + u, 1), :] = jnp.sum(
                turned_sums, axis=0, keepdims=True
            )

    @pl.loop(0, chunks)
    def _(c):
        tile(normed[piece(c), :], False)

    for level in range(levels):
        pl.semaphore_signal(
            known.at[level],
            inc=1,
            device_id=(across(1 << level),),
            device_id_type=pl.DeviceIdType.MESH,
        )
        pl.semaphore_wait(known.at[level], 1)

    @pl.loop(0, chunks)
    def _(c):
        meet(1, c)
        meet(0, c)

    for way in (1, 0):
        sums_copy(way).start()

    own = jnp.concatenate(
        [
            jnp.sum(acc[:, t * LANES : (t + 1) * LANES], axis=0, keepdims=True)
            for t in range(rows // LANES)
        ],
        axis=0,
    )
    for way in (1, 0):
        sums_copy(way).wait_recv()
    weights = 1.0 / (own + back[0] + back[1])
    part[...] = jnp.sum(weights, axis=0, keepdims=True)

    for mask in range(n - 1, 0, -1):
        pltpu.make_async_remote_copy(
            src_ref=part,
            dst_ref=parts.at[mask - 1],
            send_sem=part_send,
            recv_sem=part_recv,
            device_id=(across(mask),),
            device_id_type=pl.DeviceIdType.MESH,
        ).start()

    for way in range(2):
        sums_copy(way).wait_send()

        @pl.loop(0, chunks)
        def _(c):
            block_copy(way, c).wait_send()

    pltpu.make_async_copy(parts, parts, part_recv).wait()
    total = jnp.sum(jnp.sum(parts[...], axis=0) + part[...], axis=1, keepdims=True)
    out_ref[...] = weights * (n * rows) / total
    pltpu.make_async_copy(parts, parts, part_send).wait()


def shards(embeddings):
    n = lax.axis_size("dev")
    rows, width = embeddings.shape
    chunks = rows // CHUNK
    slabs = rows // LANES
    tiles = ROUNDS // 2 + 1
    out = pl.pallas_call(
        functools.partial(kernel, n),
        out_shape=jax.ShapeDtypeStruct((slabs, LANES), jnp.float32),
        in_specs=[pl.BlockSpec(memory_space=pl.ANY)],
        out_specs=pl.BlockSpec(memory_space=pltpu.VMEM),
        scratch_shapes=[
            pltpu.VMEM((rows, width), jnp.bfloat16),
            pltpu.VMEM((rows, width), jnp.bfloat16),
            pltpu.VMEM((width, rows), jnp.bfloat16),
            pltpu.VMEM((2, rows, width), jnp.bfloat16),
            pltpu.VMEM((8, rows), jnp.float32),
            pltpu.VMEM((2, slabs, LANES), jnp.float32),
            pltpu.VMEM((2, slabs, LANES), jnp.float32),
            pltpu.VMEM((1, LANES), jnp.float32),
            pltpu.VMEM((n - 1, 1, LANES), jnp.float32),
            pltpu.SemaphoreType.DMA((chunks,)),
            pltpu.SemaphoreType.DMA((2, chunks)),
            pltpu.SemaphoreType.DMA((2, chunks)),
            pltpu.SemaphoreType.DMA((2,)),
            pltpu.SemaphoreType.DMA((2,)),
            pltpu.SemaphoreType.DMA,
            pltpu.SemaphoreType.DMA,
            pltpu.SemaphoreType.REGULAR((n.bit_length() - 1,)),
        ],
        compiler_params=pltpu.CompilerParams(
            collective_id=0, has_side_effects=True, vmem_limit_bytes=63 * 2**20
        ),
        cost_estimate=pl.CostEstimate(
            flops=2 * tiles * rows * rows * width,
            bytes_accessed=2 * rows * width,
            transcendentals=tiles * rows * rows,
        ),
        name="pair_sums",
    )(embeddings)
    return out.reshape(rows)


def solution(mesh):
    return jax.shard_map(
        shards,
        mesh=mesh,
        in_specs=(P("dev", None),),
        out_specs=P("dev"),
        check_vma=False,
    )
```

```python
import functools
import math

import jax
import jax.numpy as jnp
from jax import lax
from jax.experimental import pallas as pl
from jax.experimental.pallas import tpu as pltpu
from jax.sharding import PartitionSpec as P

ROUNDS = 4
LANES = 128
CHUNK = 256
sharpness = 10.0


def bit_of(me, stride):
    return (me // stride) % 2


def flipped(me, stride):
    return me + stride * (1 - 2 * bit_of(me, stride))


def partners(n, me):
    top = n // 2
    found = []
    for first, second, extra in ((top, top // 2, 0), (top // 4, top // 8, 1)):
        parity = bit_of(me, first) + bit_of(me, second)
        if extra:
            parity = parity + me % 2
        parity = parity % 2
        a, b = flipped(me, first), flipped(me, second)
        target = a + parity * (b - a)
        source = b + parity * (a - b)
        found.append((target, source))
    return found


def normalize(values):
    widened = values.astype(jnp.float32)
    scaled = (
        widened
        * lax.rsqrt(jnp.mean(widened * widened, axis=1, keepdims=True) + 1e-06)
        / math.sqrt(values.shape[1])
    )
    return scaled.astype(jnp.bfloat16)


def kernel(
    n,
    emb_ref,
    out_ref,
    raw,
    normed,
    turned,
    held,
    acc,
    sums,
    back,
    part,
    parts,
    load_sem,
    send_sem,
    recv_sem,
    sums_send,
    sums_recv,
    part_send,
    part_recv,
    known,
    go,
    base,
    other,
    given,
    weights,
    base_sem,
    given_sem,
):
    rows = normed.shape[0]
    chunks = rows // CHUNK
    me = lax.axis_index("dev")

    def piece(c):
        return pl.ds(pl.multiple_of(c * CHUNK, CHUNK), CHUNK)

    def load(c):
        return pltpu.make_async_copy(
            emb_ref.at[piece(c)], raw.at[piece(c)], load_sem.at[c]
        )

    levels = n.bit_length() - 1
    flips = [flipped(me, 1 << level) - me for level in range(levels)]

    def across(mask):
        return me + sum(flips[level] for level in range(levels) if mask >> level & 1)

    barrier = pltpu.get_barrier_semaphore()
    for level in range(levels):
        pl.semaphore_signal(
            barrier,
            inc=1,
            device_id=(across(1 << level),),
            device_id_type=pl.DeviceIdType.MESH,
        )
    for c in range(chunks):
        load(c).start()

    routes = partners(n, me)
    early = (bit_of(me, n // 2) + bit_of(me, n // 4) + me % 2) % 2
    turns = (n // 2, n // 4, 1)
    acc[...] = jnp.zeros_like(acc)

    def block_copy(way, c):
        return pltpu.make_async_remote_copy(
            src_ref=normed.at[piece(c)],
            dst_ref=held.at[way, piece(c)],
            send_sem=send_sem.at[way, c],
            recv_sem=recv_sem.at[way, c],
            device_id=(routes[way][0],),
            device_id_type=pl.DeviceIdType.MESH,
        )

    def sums_copy(way):
        return pltpu.make_async_remote_copy(
            src_ref=sums.at[way],
            dst_ref=back.at[way],
            send_sem=sums_send.at[way],
            recv_sem=sums_recv.at[way],
            device_id=(routes[way][1],),
            device_id_type=pl.DeviceIdType.MESH,
        )

    def prepare(c):
        load(c).wait()
        normed[piece(c), :] = normalize(raw[piece(c), :])

    def turn(c):
        turned[:, piece(c)] = normed[piece(c), :].T

    prepare(0)
    pl.semaphore_wait(barrier, levels)
    for c in range(chunks):
        if c:
            prepare(c)
        block_copy(1, c).start()

        @pl.when(early == 1)
        def _():
            block_copy(0, c).start()

    for c in range(chunks):
        turn(c)

    def tile(block, fold):
        folded = None
        for t in range(chunks):
            columns = slice(t * CHUNK, (t + 1) * CHUNK)
            similarity = jnp.dot(
                block, turned[:, columns], preferred_element_type=jnp.float32
            )
            values = jnp.exp(sharpness * (similarity - 1.0))
            acc[:, columns] += jnp.sum(
                values.reshape(CHUNK // 8, 8, CHUNK), axis=0
            )
            if fold:
                for u in range(0, CHUNK, LANES):
                    term = values[:, u : u + LANES]
                    folded = term if folded is None else folded + term
        return folded

    def meet(way, c):
        block_copy(way, c).wait_recv()
        folded = tile(held[way, piece(c), :], True)
        for u in range(CHUNK // LANES):
            turned_sums = folded[u * LANES : (u + 1) * LANES].T
            sums[way, pl.ds(c * (CHUNK // LANES) + u, 1), :] = jnp.sum(
                turned_sums, axis=0, keepdims=True
            )

    @pl.loop(0, chunks)
    def _(c):
        tile(normed[piece(c), :], False)

    for level in range(levels):
        pl.semaphore_signal(
            known.at[level],
            inc=1,
            device_id=(across(1 << level),),
            device_id_type=pl.DeviceIdType.MESH,
        )
        pl.semaphore_wait(known.at[level], 1)

    @pl.when(early == 1)
    def _():
        for c in range(chunks - 1):
            block_copy(0, c).wait_send()
        pl.semaphore_signal(
            go,
            inc=1,
            device_id=(across(1),),
            device_id_type=pl.DeviceIdType.MESH,
        )

    @pl.when(early == 0)
    def _():
        @pl.loop(0, chunks - 1)
        def _(c):
            meet(0, c)

        pl.semaphore_wait(go, 1)
        for c in range(chunks):
            block_copy(0, c).start()
        meet(0, chunks - 1)
        sums_copy(0).start()

    @pl.loop(0, chunks)
    def _(c):
        meet(1, c)

    sums_copy(1).start()

    def own():
        return jnp.concatenate(
            [
                jnp.sum(acc[:, t * LANES : (t + 1) * LANES], axis=0, keepdims=True)
                for t in range(rows // LANES)
            ],
            axis=0,
        )

    def plain_copy(src, dst, pair, device):
        return pltpu.make_async_remote_copy(
            src_ref=src,
            dst_ref=dst,
            send_sem=pair.at[0],
            recv_sem=pair.at[1],
            device_id=(device,),
            device_id_type=pl.DeviceIdType.MESH,
        )

    base_copy = plain_copy(base, other, base_sem, routes[0][0])
    given_copy = plain_copy(given, weights, given_sem, routes[0][1])

    kinds = ([], [])
    for mask in range(n - 1, 0, -1):
        kinds[sum(1 for turn in turns if mask & turn) % 2].append(mask)
    same = len(kinds[0])

    sums_copy(1).wait_recv()

    @pl.when(early == 0)
    def _():
        base[...] = own() + back[1]
        base_copy.start()
        given_copy.wait_recv()
        pltpu.make_async_copy(parts, parts, part_recv).wait()
        base_copy.wait_send()
        sums_copy(0).wait_send()
        for c in range(chunks):
            block_copy(0, c).wait_send()

    @pl.when(early == 1)
    def _():
        sums_copy(0).wait_recv()
        base_copy.wait_recv()

        @pl.loop(0, chunks)
        def _(c):
            meet(0, c)

        theirs = 1.0 / (other[...] + sums[0])
        mine = 1.0 / (own() + back[0] + back[1])
        given[...] = theirs
        weights[...] = mine
        part[...] = jnp.sum(theirs + mine, axis=0, keepdims=True)
        given_copy.start()
        for kind in (1, 0):
            for slot, mask in enumerate(kinds[kind]):
                pltpu.make_async_remote_copy(
                    src_ref=part,
                    dst_ref=parts.at[slot],
                    send_sem=part_send.at[kind],
                    recv_sem=part_recv,
                    device_id=(across(mask),),
                    device_id_type=pl.DeviceIdType.MESH,
                ).start()
        parts[same] = part[...]
        head = parts.at[pl.ds(0, same)]
        pltpu.make_async_copy(head, head, part_recv).wait()
        given_copy.wait_send()
        block_copy(0, chunks - 1).wait_send()
        pltpu.make_async_copy(head, head, part_send.at[0]).wait()
        pltpu.make_async_copy(parts, parts, part_send.at[1]).wait()

    sums_copy(1).wait_send()
    for c in range(chunks):
        block_copy(1, c).wait_send()
    total = jnp.sum(jnp.sum(parts[...], axis=0), axis=1, keepdims=True)
    out_ref[...] = weights[...] * (n * rows) / total


def shards(embeddings):
    n = lax.axis_size("dev")
    rows, width = embeddings.shape
    chunks = rows // CHUNK
    slabs = rows // LANES
    tiles = ROUNDS // 2 + 1
    out = pl.pallas_call(
        functools.partial(kernel, n),
        out_shape=jax.ShapeDtypeStruct((slabs, LANES), jnp.float32),
        in_specs=[pl.BlockSpec(memory_space=pl.ANY)],
        out_specs=pl.BlockSpec(memory_space=pltpu.VMEM),
        scratch_shapes=[
            pltpu.VMEM((rows, width), jnp.bfloat16),
            pltpu.VMEM((rows, width), jnp.bfloat16),
            pltpu.VMEM((width, rows), jnp.bfloat16),
            pltpu.VMEM((2, rows, width), jnp.bfloat16),
            pltpu.VMEM((8, rows), jnp.float32),
            pltpu.VMEM((2, slabs, LANES), jnp.float32),
            pltpu.VMEM((2, slabs, LANES), jnp.float32),
            pltpu.VMEM((1, LANES), jnp.float32),
            pltpu.VMEM((n // 2, 1, LANES), jnp.float32),
            pltpu.SemaphoreType.DMA((chunks,)),
            pltpu.SemaphoreType.DMA((2, chunks)),
            pltpu.SemaphoreType.DMA((2, chunks)),
            pltpu.SemaphoreType.DMA((2,)),
            pltpu.SemaphoreType.DMA((2,)),
            pltpu.SemaphoreType.DMA((2,)),
            pltpu.SemaphoreType.DMA,
            pltpu.SemaphoreType.REGULAR((n.bit_length() - 1,)),
            pltpu.SemaphoreType.REGULAR,
            pltpu.VMEM((slabs, LANES), jnp.float32),
            pltpu.VMEM((slabs, LANES), jnp.float32),
            pltpu.VMEM((slabs, LANES), jnp.float32),
            pltpu.VMEM((slabs, LANES), jnp.float32),
            pltpu.SemaphoreType.DMA((2,)),
            pltpu.SemaphoreType.DMA((2,)),
        ],
        compiler_params=pltpu.CompilerParams(
            collective_id=0, has_side_effects=True, vmem_limit_bytes=63 * 2**20
        ),
        cost_estimate=pl.CostEstimate(
            flops=2 * tiles * rows * rows * width,
            bytes_accessed=2 * rows * width,
            transcendentals=tiles * rows * rows,
        ),
        name="pair_sums",
    )(embeddings)
    return out.reshape(rows)


def solution(mesh):
    return jax.shard_map(
        shards,
        mesh=mesh,
        in_specs=(P("dev", None),),
        out_specs=P("dev"),
        check_vma=False,
    )
```

```python
import functools
import math

import jax
import jax.numpy as jnp
from jax import lax
from jax.experimental import pallas as pl
from jax.experimental.pallas import tpu as pltpu
from jax.sharding import PartitionSpec as P

ROUNDS = 4
LANES = 128
CHUNK = 256
sharpness = 10.0


def bit_of(me, stride):
    return (me // stride) % 2


def flipped(me, stride):
    return me + stride * (1 - 2 * bit_of(me, stride))


def partners(n, me):
    top = n // 2
    found = []
    for first, second, extra in ((top, top // 2, 0), (top // 4, top // 8, 1)):
        parity = bit_of(me, first) + bit_of(me, second)
        if extra:
            parity = parity + me % 2
        parity = parity % 2
        a, b = flipped(me, first), flipped(me, second)
        target = a + parity * (b - a)
        source = b + parity * (a - b)
        found.append((target, source))
    return found


def normalize(values):
    widened = values.astype(jnp.float32)
    scaled = (
        widened
        * lax.rsqrt(jnp.mean(widened * widened, axis=1, keepdims=True) + 1e-06)
        / math.sqrt(values.shape[1])
    )
    return scaled.astype(jnp.bfloat16)


def kernel(
    n,
    emb_ref,
    out_ref,
    raw,
    normed,
    turned,
    held,
    acc,
    sums,
    back,
    part,
    parts,
    load_sem,
    send_sem,
    recv_sem,
    sums_send,
    sums_recv,
    part_send,
    part_recv,
    known,
    go,
    base,
    other,
    given,
    weights,
    base_sem,
    given_sem,
):
    rows = normed.shape[0]
    chunks = rows // CHUNK
    me = lax.axis_index("dev")

    def piece(c):
        return pl.ds(pl.multiple_of(c * CHUNK, CHUNK), CHUNK)

    def load(c):
        return pltpu.make_async_copy(
            emb_ref.at[piece(c)], raw.at[piece(c)], load_sem.at[c]
        )

    levels = n.bit_length() - 1
    flips = [flipped(me, 1 << level) - me for level in range(levels)]

    def across(mask):
        return me + sum(flips[level] for level in range(levels) if mask >> level & 1)

    barrier = pltpu.get_barrier_semaphore()
    for level in range(levels):
        pl.semaphore_signal(
            barrier,
            inc=1,
            device_id=(across(1 << level),),
            device_id_type=pl.DeviceIdType.MESH,
        )
    for c in range(chunks):
        load(c).start()

    routes = partners(n, me)
    early = (bit_of(me, n // 2) + bit_of(me, n // 4) + me % 2) % 2
    turns = (n // 2, n // 4, 1)
    acc[...] = jnp.zeros_like(acc)

    def block_copy(way, c):
        return pltpu.make_async_remote_copy(
            src_ref=normed.at[piece(c)],
            dst_ref=held.at[way, piece(c)],
            send_sem=send_sem.at[way, c],
            recv_sem=recv_sem.at[way, c],
            device_id=(routes[way][0],),
            device_id_type=pl.DeviceIdType.MESH,
        )

    def sums_copy(way):
        return pltpu.make_async_remote_copy(
            src_ref=sums.at[way],
            dst_ref=back.at[way],
            send_sem=sums_send.at[way],
            recv_sem=sums_recv.at[way],
            device_id=(routes[way][1],),
            device_id_type=pl.DeviceIdType.MESH,
        )

    def prepare(c):
        load(c).wait()
        normed[piece(c), :] = normalize(raw[piece(c), :])

    def turn(c):
        turned[:, piece(c)] = normed[piece(c), :].T

    prepare(0)
    pl.semaphore_wait(barrier, levels)
    for c in range(chunks):
        if c:
            prepare(c)

        @pl.when(early == 1)
        def _():
            block_copy(0, c).start()

        block_copy(1, c).start()

    for c in range(chunks):
        turn(c)

    def tile(block, fold):
        folded = None
        for t in range(chunks):
            columns = slice(t * CHUNK, (t + 1) * CHUNK)
            similarity = jnp.dot(
                block, turned[:, columns], preferred_element_type=jnp.float32
            )
            values = jnp.exp(sharpness * (similarity - 1.0))
            acc[:, columns] += jnp.sum(
                values.reshape(CHUNK // 8, 8, CHUNK), axis=0
            )
            if fold:
                for u in range(0, CHUNK, LANES):
                    term = values[:, u : u + LANES]
                    folded = term if folded is None else folded + term
        return folded

    def meet(way, c):
        block_copy(way, c).wait_recv()
        folded = tile(held[way, piece(c), :], True)
        for u in range(CHUNK // LANES):
            turned_sums = folded[u * LANES : (u + 1) * LANES].T
            sums[way, pl.ds(c * (CHUNK // LANES) + u, 1), :] = jnp.sum(
                turned_sums, axis=0, keepdims=True
            )

    @pl.loop(0, chunks)
    def _(c):
        tile(normed[piece(c), :], False)

    for level in range(levels):
        pl.semaphore_signal(
            known.at[level],
            inc=1,
            device_id=(across(1 << level),),
            device_id_type=pl.DeviceIdType.MESH,
        )
        pl.semaphore_wait(known.at[level], 1)

    @pl.when(early == 1)
    def _():
        for c in range(chunks - 2):
            block_copy(0, c).wait_send()
        pl.semaphore_signal(
            go,
            inc=1,
            device_id=(across(1),),
            device_id_type=pl.DeviceIdType.MESH,
        )

    @pl.when(early == 0)
    def _():
        pl.semaphore_wait(go, 1)
        for c in range(chunks):
            block_copy(0, c).start()

        @pl.loop(0, chunks)
        def _(c):
            meet(0, c)

        sums_copy(0).start()

    @pl.loop(0, chunks)
    def _(c):
        meet(1, c)

    sums_copy(1).start()

    def own():
        return jnp.concatenate(
            [
                jnp.sum(acc[:, t * LANES : (t + 1) * LANES], axis=0, keepdims=True)
                for t in range(rows // LANES)
            ],
            axis=0,
        )

    def plain_copy(src, dst, pair, device):
        return pltpu.make_async_remote_copy(
            src_ref=src,
            dst_ref=dst,
            send_sem=pair.at[0],
            recv_sem=pair.at[1],
            device_id=(device,),
            device_id_type=pl.DeviceIdType.MESH,
        )

    base_copy = plain_copy(base, other, base_sem, routes[0][0])
    given_copy = plain_copy(given, weights, given_sem, routes[0][1])

    kinds = ([], [])
    for mask in range(n - 1, 0, -1):
        kinds[sum(1 for turn in turns if mask & turn) % 2].append(mask)
    same = len(kinds[0])

    sums_copy(1).wait_recv()

    @pl.when(early == 0)
    def _():
        base[...] = own() + back[1]
        base_copy.start()
        given_copy.wait_recv()
        pltpu.make_async_copy(parts, parts, part_recv).wait()
        base_copy.wait_send()
        sums_copy(0).wait_send()
        for c in range(chunks):
            block_copy(0, c).wait_send()

    @pl.when(early == 1)
    def _():
        sums_copy(0).wait_recv()
        base_copy.wait_recv()

        @pl.loop(0, chunks)
        def _(c):
            meet(0, c)

        theirs = 1.0 / (other[...] + sums[0])
        mine = 1.0 / (own() + back[0] + back[1])
        given[...] = theirs
        weights[...] = mine
        part[...] = jnp.sum(theirs + mine, axis=0, keepdims=True)
        given_copy.start()
        for kind in (1, 0):
            for slot, mask in enumerate(kinds[kind]):
                pltpu.make_async_remote_copy(
                    src_ref=part,
                    dst_ref=parts.at[slot],
                    send_sem=part_send.at[kind],
                    recv_sem=part_recv,
                    device_id=(across(mask),),
                    device_id_type=pl.DeviceIdType.MESH,
                ).start()
        parts[same] = part[...]
        head = parts.at[pl.ds(0, same)]
        pltpu.make_async_copy(head, head, part_recv).wait()
        given_copy.wait_send()
        for c in range(chunks - 2, chunks):
            block_copy(0, c).wait_send()
        pltpu.make_async_copy(head, head, part_send.at[0]).wait()
        pltpu.make_async_copy(parts, parts, part_send.at[1]).wait()

    sums_copy(1).wait_send()
    for c in range(chunks):
        block_copy(1, c).wait_send()
    total = jnp.sum(jnp.sum(parts[...], axis=0), axis=1, keepdims=True)
    out_ref[...] = weights[...] * (n * rows) / total


def shards(embeddings):
    n = lax.axis_size("dev")
    rows, width = embeddings.shape
    chunks = rows // CHUNK
    slabs = rows // LANES
    tiles = ROUNDS // 2 + 1
    out = pl.pallas_call(
        functools.partial(kernel, n),
        out_shape=jax.ShapeDtypeStruct((slabs, LANES), jnp.float32),
        in_specs=[pl.BlockSpec(memory_space=pl.ANY)],
        out_specs=pl.BlockSpec(memory_space=pltpu.VMEM),
        scratch_shapes=[
            pltpu.VMEM((rows, width), jnp.bfloat16),
            pltpu.VMEM((rows, width), jnp.bfloat16),
            pltpu.VMEM((width, rows), jnp.bfloat16),
            pltpu.VMEM((2, rows, width), jnp.bfloat16),
            pltpu.VMEM((8, rows), jnp.float32),
            pltpu.VMEM((2, slabs, LANES), jnp.float32),
            pltpu.VMEM((2, slabs, LANES), jnp.float32),
            pltpu.VMEM((1, LANES), jnp.float32),
            pltpu.VMEM((n // 2, 1, LANES), jnp.float32),
            pltpu.SemaphoreType.DMA((chunks,)),
            pltpu.SemaphoreType.DMA((2, chunks)),
            pltpu.SemaphoreType.DMA((2, chunks)),
            pltpu.SemaphoreType.DMA((2,)),
            pltpu.SemaphoreType.DMA((2,)),
            pltpu.SemaphoreType.DMA((2,)),
            pltpu.SemaphoreType.DMA,
            pltpu.SemaphoreType.REGULAR((n.bit_length() - 1,)),
            pltpu.SemaphoreType.REGULAR,
            pltpu.VMEM((slabs, LANES), jnp.float32),
            pltpu.VMEM((slabs, LANES), jnp.float32),
            pltpu.VMEM((slabs, LANES), jnp.float32),
            pltpu.VMEM((slabs, LANES), jnp.float32),
            pltpu.SemaphoreType.DMA((2,)),
            pltpu.SemaphoreType.DMA((2,)),
        ],
        compiler_params=pltpu.CompilerParams(
            collective_id=0, has_side_effects=True, vmem_limit_bytes=63 * 2**20
        ),
        cost_estimate=pl.CostEstimate(
            flops=2 * tiles * rows * rows * width,
            bytes_accessed=2 * rows * width,
            transcendentals=tiles * rows * rows,
        ),
        name="pair_sums",
    )(embeddings)
    return out.reshape(rows)


def solution(mesh):
    return jax.shard_map(
        shards,
        mesh=mesh,
        in_specs=(P("dev", None),),
        out_specs=P("dev"),
        check_vma=False,
    )
```

```python
import functools
import math

import jax
import jax.numpy as jnp
from jax import lax
from jax.experimental import pallas as pl
from jax.experimental.pallas import tpu as pltpu
from jax.sharding import PartitionSpec as P

ROUNDS = 4
LANES = 128
CHUNK = 128
PART = 256
sharpness = 10.0


def bit_of(me, stride):
    return (me // stride) % 2


def flipped(me, stride):
    return me + stride * (1 - 2 * bit_of(me, stride))


def partners(n, me):
    top = n // 2
    found = []
    for first, second, extra in ((top, top // 2, 0), (top // 4, top // 8, 1)):
        parity = bit_of(me, first) + bit_of(me, second)
        if extra:
            parity = parity + me % 2
        parity = parity % 2
        a, b = flipped(me, first), flipped(me, second)
        target = a + parity * (b - a)
        source = b + parity * (a - b)
        found.append((target, source))
    return found


def normalize(values):
    widened = values.astype(jnp.float32)
    scaled = (
        widened
        * lax.rsqrt(jnp.mean(widened * widened, axis=1, keepdims=True) + 1e-06)
        / math.sqrt(values.shape[1])
    )
    return scaled.astype(jnp.bfloat16)


def kernel(
    n,
    emb_ref,
    out_ref,
    raw,
    normed,
    turned,
    held,
    acc,
    sums,
    back,
    part,
    parts,
    load_sem,
    send_sem,
    recv_sem,
    sums_send,
    sums_recv,
    part_send,
    part_recv,
    known,
    go,
    base,
    other,
    given,
    weights,
    base_sem,
    given_sem,
):
    rows = normed.shape[0]
    chunks = rows // CHUNK
    me = lax.axis_index("dev")

    def piece(c):
        return pl.ds(pl.multiple_of(c * CHUNK, CHUNK), CHUNK)

    def load(c):
        return pltpu.make_async_copy(
            emb_ref.at[piece(c)], raw.at[piece(c)], load_sem.at[c]
        )

    levels = n.bit_length() - 1
    flips = [flipped(me, 1 << level) - me for level in range(levels)]

    def across(mask):
        return me + sum(flips[level] for level in range(levels) if mask >> level & 1)

    barrier = pltpu.get_barrier_semaphore()
    for level in range(levels):
        pl.semaphore_signal(
            barrier,
            inc=1,
            device_id=(across(1 << level),),
            device_id_type=pl.DeviceIdType.MESH,
        )
    for c in range(chunks):
        load(c).start()

    routes = partners(n, me)
    early = (bit_of(me, n // 2) + bit_of(me, n // 4) + me % 2) % 2
    turns = (n // 2, n // 4, 1)
    acc[...] = jnp.zeros_like(acc)

    def block_copy(way, c):
        return pltpu.make_async_remote_copy(
            src_ref=normed.at[piece(c)],
            dst_ref=held.at[way, piece(c)],
            send_sem=send_sem.at[way, c],
            recv_sem=recv_sem.at[way, c],
            device_id=(routes[way][0],),
            device_id_type=pl.DeviceIdType.MESH,
        )

    def sums_copy(way):
        return pltpu.make_async_remote_copy(
            src_ref=sums.at[way],
            dst_ref=back.at[way],
            send_sem=sums_send.at[way],
            recv_sem=sums_recv.at[way],
            device_id=(routes[way][1],),
            device_id_type=pl.DeviceIdType.MESH,
        )

    def prepare(c):
        load(c).wait()
        normed[piece(c), :] = normalize(raw[piece(c), :])

    def turn(c):
        turned[:, piece(c)] = normed[piece(c), :].T

    prepare(0)
    pl.semaphore_wait(barrier, levels)
    for c in range(chunks):
        if c:
            prepare(c)

        @pl.when(early == 1)
        def _():
            block_copy(0, c).start()

        block_copy(1, c).start()

    for c in range(chunks):
        turn(c)

    def tile(block, fold):
        folded = None
        for t in range(rows // PART):
            columns = slice(t * PART, (t + 1) * PART)
            similarity = jnp.dot(
                block, turned[:, columns], preferred_element_type=jnp.float32
            )
            values = jnp.exp(sharpness * (similarity - 1.0))
            acc[:, columns] += jnp.sum(
                values.reshape(CHUNK // 8, 8, PART), axis=0
            )
            if fold:
                for u in range(0, PART, LANES):
                    term = values[:, u : u + LANES]
                    folded = term if folded is None else folded + term
        return folded

    def meet(way, c):
        block_copy(way, c).wait_recv()
        folded = tile(held[way, piece(c), :], True)
        for u in range(CHUNK // LANES):
            turned_sums = folded[u * LANES : (u + 1) * LANES].T
            sums[way, pl.ds(c * (CHUNK // LANES) + u, 1), :] = jnp.sum(
                turned_sums, axis=0, keepdims=True
            )

    @pl.loop(0, chunks)
    def _(c):
        tile(normed[piece(c), :], False)

    for level in range(levels):
        pl.semaphore_signal(
            known.at[level],
            inc=1,
            device_id=(across(1 << level),),
            device_id_type=pl.DeviceIdType.MESH,
        )
        pl.semaphore_wait(known.at[level], 1)

    @pl.when(early == 1)
    def _():
        for c in range(chunks // 2):
            block_copy(0, c).wait_send()
        pl.semaphore_signal(
            go,
            inc=1,
            device_id=(across(1),),
            device_id_type=pl.DeviceIdType.MESH,
        )

    @pl.when(early == 0)
    def _():
        pl.semaphore_wait(go, 1)
        for c in range(chunks):
            block_copy(0, c).start()

        @pl.loop(0, chunks)
        def _(c):
            meet(0, c)

        sums_copy(0).start()

    @pl.loop(0, chunks)
    def _(c):
        meet(1, c)

    sums_copy(1).start()

    def own():
        return jnp.concatenate(
            [
                jnp.sum(acc[:, t * LANES : (t + 1) * LANES], axis=0, keepdims=True)
                for t in range(rows // LANES)
            ],
            axis=0,
        )

    def plain_copy(src, dst, pair, device):
        return pltpu.make_async_remote_copy(
            src_ref=src,
            dst_ref=dst,
            send_sem=pair.at[0],
            recv_sem=pair.at[1],
            device_id=(device,),
            device_id_type=pl.DeviceIdType.MESH,
        )

    base_copy = plain_copy(base, other, base_sem, routes[0][0])
    given_copy = plain_copy(given, weights, given_sem, routes[0][1])

    kinds = ([], [])
    for mask in range(n - 1, 0, -1):
        kinds[sum(1 for turn in turns if mask & turn) % 2].append(mask)
    same = len(kinds[0])

    sums_copy(1).wait_recv()

    @pl.when(early == 0)
    def _():
        base[...] = own() + back[1]
        base_copy.start()
        given_copy.wait_recv()
        pltpu.make_async_copy(parts, parts, part_recv).wait()
        base_copy.wait_send()
        sums_copy(0).wait_send()
        for c in range(chunks):
            block_copy(0, c).wait_send()

    @pl.when(early == 1)
    def _():
        sums_copy(0).wait_recv()
        base_copy.wait_recv()

        @pl.loop(0, chunks)
        def _(c):
            meet(0, c)

        theirs = 1.0 / (other[...] + sums[0])
        mine = 1.0 / (own() + back[0] + back[1])
        given[...] = theirs
        weights[...] = mine
        part[...] = jnp.sum(theirs + mine, axis=0, keepdims=True)
        given_copy.start()
        for kind in (1, 0):
            for slot, mask in enumerate(kinds[kind]):
                pltpu.make_async_remote_copy(
                    src_ref=part,
                    dst_ref=parts.at[slot],
                    send_sem=part_send.at[kind],
                    recv_sem=part_recv,
                    device_id=(across(mask),),
                    device_id_type=pl.DeviceIdType.MESH,
                ).start()
        parts[same] = part[...]
        head = parts.at[pl.ds(0, same)]
        pltpu.make_async_copy(head, head, part_recv).wait()
        given_copy.wait_send()
        for c in range(chunks // 2, chunks):
            block_copy(0, c).wait_send()
        pltpu.make_async_copy(head, head, part_send.at[0]).wait()
        pltpu.make_async_copy(parts, parts, part_send.at[1]).wait()

    sums_copy(1).wait_send()
    for c in range(chunks):
        block_copy(1, c).wait_send()
    total = jnp.sum(jnp.sum(parts[...], axis=0), axis=1, keepdims=True)
    out_ref[...] = weights[...] * (n * rows) / total


def shards(embeddings):
    n = lax.axis_size("dev")
    rows, width = embeddings.shape
    chunks = rows // CHUNK
    slabs = rows // LANES
    tiles = ROUNDS // 2 + 1
    out = pl.pallas_call(
        functools.partial(kernel, n),
        out_shape=jax.ShapeDtypeStruct((slabs, LANES), jnp.float32),
        in_specs=[pl.BlockSpec(memory_space=pl.ANY)],
        out_specs=pl.BlockSpec(memory_space=pltpu.VMEM),
        scratch_shapes=[
            pltpu.VMEM((rows, width), jnp.bfloat16),
            pltpu.VMEM((rows, width), jnp.bfloat16),
            pltpu.VMEM((width, rows), jnp.bfloat16),
            pltpu.VMEM((2, rows, width), jnp.bfloat16),
            pltpu.VMEM((8, rows), jnp.float32),
            pltpu.VMEM((2, slabs, LANES), jnp.float32),
            pltpu.VMEM((2, slabs, LANES), jnp.float32),
            pltpu.VMEM((1, LANES), jnp.float32),
            pltpu.VMEM((n // 2, 1, LANES), jnp.float32),
            pltpu.SemaphoreType.DMA((chunks,)),
            pltpu.SemaphoreType.DMA((2, chunks)),
            pltpu.SemaphoreType.DMA((2, chunks)),
            pltpu.SemaphoreType.DMA((2,)),
            pltpu.SemaphoreType.DMA((2,)),
            pltpu.SemaphoreType.DMA((2,)),
            pltpu.SemaphoreType.DMA,
            pltpu.SemaphoreType.REGULAR((n.bit_length() - 1,)),
            pltpu.SemaphoreType.REGULAR,
            pltpu.VMEM((slabs, LANES), jnp.float32),
            pltpu.VMEM((slabs, LANES), jnp.float32),
            pltpu.VMEM((slabs, LANES), jnp.float32),
            pltpu.VMEM((slabs, LANES), jnp.float32),
            pltpu.SemaphoreType.DMA((2,)),
            pltpu.SemaphoreType.DMA((2,)),
        ],
        compiler_params=pltpu.CompilerParams(
            collective_id=0, has_side_effects=True, vmem_limit_bytes=63 * 2**20
        ),
        cost_estimate=pl.CostEstimate(
            flops=2 * tiles * rows * rows * width,
            bytes_accessed=2 * rows * width,
            transcendentals=tiles * rows * rows,
        ),
        name="pair_sums",
    )(embeddings)
    return out.reshape(rows)


def solution(mesh):
    return jax.shard_map(
        shards,
        mesh=mesh,
        in_specs=(P("dev", None),),
        out_specs=P("dev"),
        check_vma=False,
    )
```

```python
import functools
import math

import jax
import jax.numpy as jnp
from jax import lax
from jax.experimental import pallas as pl
from jax.experimental.pallas import tpu as pltpu
from jax.sharding import PartitionSpec as P

ROUNDS = 4
LANES = 128
CHUNK = 256
sharpness = 10.0


def bit_of(me, stride):
    return (me // stride) % 2


def flipped(me, stride):
    return me + stride * (1 - 2 * bit_of(me, stride))


def partners(n, me):
    top = n // 2
    found = []
    for first, second, extra in ((top, top // 2, 0), (top // 4, top // 8, 1)):
        parity = bit_of(me, first) + bit_of(me, second)
        if extra:
            parity = parity + me % 2
        parity = parity % 2
        a, b = flipped(me, first), flipped(me, second)
        target = a + parity * (b - a)
        source = b + parity * (a - b)
        found.append((target, source))
    return found


def normalize(values):
    widened = values.astype(jnp.float32)
    scaled = (
        widened
        * lax.rsqrt(jnp.mean(widened * widened, axis=1, keepdims=True) + 1e-06)
        / math.sqrt(values.shape[1])
    )
    return scaled.astype(jnp.bfloat16)


def kernel(
    n,
    emb_ref,
    out_ref,
    raw,
    normed,
    turned,
    held,
    acc,
    sums,
    back,
    part,
    parts,
    load_sem,
    send_sem,
    recv_sem,
    sums_send,
    sums_recv,
    part_send,
    part_recv,
    known,
    go,
    base,
    other,
    given,
    weights,
    base_sem,
    given_sem,
):
    rows = normed.shape[0]
    chunks = rows // CHUNK
    me = lax.axis_index("dev")

    def piece(c):
        return pl.ds(pl.multiple_of(c * CHUNK, CHUNK), CHUNK)

    def load(c):
        return pltpu.make_async_copy(
            emb_ref.at[piece(c)], raw.at[piece(c)], load_sem.at[c]
        )

    levels = n.bit_length() - 1
    flips = [flipped(me, 1 << level) - me for level in range(levels)]

    def across(mask):
        return me + sum(flips[level] for level in range(levels) if mask >> level & 1)

    barrier = pltpu.get_barrier_semaphore()
    for level in range(levels):
        pl.semaphore_signal(
            barrier,
            inc=1,
            device_id=(across(1 << level),),
            device_id_type=pl.DeviceIdType.MESH,
        )
    for c in range(chunks):
        load(c).start()

    routes = partners(n, me)
    early = (bit_of(me, n // 2) + bit_of(me, n // 4) + me % 2) % 2
    turns = (n // 2, n // 4, 1)
    acc[...] = jnp.zeros_like(acc)

    def block_copy(way, c):
        return pltpu.make_async_remote_copy(
            src_ref=normed.at[piece(c)],
            dst_ref=held.at[way, piece(c)],
            send_sem=send_sem.at[way, c],
            recv_sem=recv_sem.at[way, c],
            device_id=(routes[way][0],),
            device_id_type=pl.DeviceIdType.MESH,
        )

    def sums_copy(way):
        return pltpu.make_async_remote_copy(
            src_ref=sums.at[way],
            dst_ref=back.at[way],
            send_sem=sums_send.at[way],
            recv_sem=sums_recv.at[way],
            device_id=(routes[way][1],),
            device_id_type=pl.DeviceIdType.MESH,
        )

    def prepare(c):
        load(c).wait()
        normed[piece(c), :] = normalize(raw[piece(c), :])

    def turn(c):
        turned[:, piece(c)] = normed[piece(c), :].T

    prepare(0)
    pl.semaphore_wait(barrier, levels)
    for c in range(chunks):
        if c:
            prepare(c)

        @pl.when(early == 1)
        def _():
            block_copy(0, c).start()

        block_copy(1, c).start()

    for c in range(chunks):
        turn(c)

    def tile(block, fold):
        folded = None
        for t in range(chunks):
            columns = slice(t * CHUNK, (t + 1) * CHUNK)
            similarity = jnp.dot(
                block, turned[:, columns], preferred_element_type=jnp.float32
            )
            values = jnp.exp(sharpness * (similarity - 1.0))
            acc[:, columns] += jnp.sum(
                values.reshape(CHUNK // 8, 8, CHUNK), axis=0
            )
            if fold:
                for u in range(0, CHUNK, LANES):
                    term = values[:, u : u + LANES]
                    folded = term if folded is None else folded + term
        return folded

    def meet(way, c):
        block_copy(way, c).wait_recv()
        folded = tile(held[way, piece(c), :], True)
        for u in range(CHUNK // LANES):
            turned_sums = folded[u * LANES : (u + 1) * LANES].T
            sums[way, pl.ds(c * (CHUNK // LANES) + u, 1), :] = jnp.sum(
                turned_sums, axis=0, keepdims=True
            )

    @pl.loop(0, chunks)
    def _(c):
        tile(normed[piece(c), :], False)

    for level in range(levels):
        pl.semaphore_signal(
            known.at[level],
            inc=1,
            device_id=(across(1 << level),),
            device_id_type=pl.DeviceIdType.MESH,
        )
        pl.semaphore_wait(known.at[level], 1)

    @pl.when(early == 1)
    def _():
        for c in range(chunks - 2):
            block_copy(0, c).wait_send()
        pl.semaphore_signal(
            go,
            inc=1,
            device_id=(across(1),),
            device_id_type=pl.DeviceIdType.MESH,
        )

    @pl.when(early == 0)
    def _():
        pl.semaphore_wait(go, 1)
        for c in range(chunks):
            block_copy(0, c).start()

        @pl.loop(0, chunks)
        def _(c):
            meet(0, c)

        sums_copy(0).start()

    @pl.loop(0, chunks)
    def _(c):
        meet(1, c)

    sums_copy(1).start()

    def own():
        return jnp.concatenate(
            [
                jnp.sum(acc[:, t * LANES : (t + 1) * LANES], axis=0, keepdims=True)
                for t in range(rows // LANES)
            ],
            axis=0,
        )

    def plain_copy(src, dst, pair, device):
        return pltpu.make_async_remote_copy(
            src_ref=src,
            dst_ref=dst,
            send_sem=pair.at[0],
            recv_sem=pair.at[1],
            device_id=(device,),
            device_id_type=pl.DeviceIdType.MESH,
        )

    base_copy = plain_copy(base, other, base_sem, routes[0][0])
    given_copy = plain_copy(given, weights, given_sem, routes[0][1])

    kinds = ([], [])
    for mask in range(n - 1, 0, -1):
        kinds[sum(1 for turn in turns if mask & turn) % 2].append(mask)
    same = len(kinds[0])

    @pl.when(early == 0)
    def _():
        sums_copy(1).wait_recv()
        base[...] = own() + back[1]
        base_copy.start()
        given_copy.wait_recv()
        pltpu.make_async_copy(parts, parts, part_recv).wait()
        base_copy.wait_send()
        sums_copy(0).wait_send()
        for c in range(chunks):
            block_copy(0, c).wait_send()

    @pl.when(early == 1)
    def _():
        @pl.loop(0, chunks)
        def _(c):
            meet(0, c)

        for way in range(2):
            sums_copy(way).wait_recv()
        base_copy.wait_recv()
        theirs = 1.0 / (other[...] + sums[0])
        mine = 1.0 / (own() + back[0] + back[1])
        given[...] = theirs
        weights[...] = mine
        part[...] = jnp.sum(theirs + mine, axis=0, keepdims=True)
        given_copy.start()
        for kind in (1, 0):
            for slot, mask in enumerate(kinds[kind]):
                pltpu.make_async_remote_copy(
                    src_ref=part,
                    dst_ref=parts.at[slot],
                    send_sem=part_send.at[kind],
                    recv_sem=part_recv,
                    device_id=(across(mask),),
                    device_id_type=pl.DeviceIdType.MESH,
                ).start()
        parts[same] = part[...]
        head = parts.at[pl.ds(0, same)]
        pltpu.make_async_copy(head, head, part_recv).wait()
        given_copy.wait_send()
        for c in range(chunks - 2, chunks):
            block_copy(0, c).wait_send()
        pltpu.make_async_copy(head, head, part_send.at[0]).wait()
        pltpu.make_async_copy(parts, parts, part_send.at[1]).wait()

    sums_copy(1).wait_send()
    for c in range(chunks):
        block_copy(1, c).wait_send()
    total = jnp.sum(jnp.sum(parts[...], axis=0), axis=1, keepdims=True)
    out_ref[...] = weights[...] * (n * rows) / total


def shards(embeddings):
    n = lax.axis_size("dev")
    rows, width = embeddings.shape
    chunks = rows // CHUNK
    slabs = rows // LANES
    tiles = ROUNDS // 2 + 1
    out = pl.pallas_call(
        functools.partial(kernel, n),
        out_shape=jax.ShapeDtypeStruct((slabs, LANES), jnp.float32),
        in_specs=[pl.BlockSpec(memory_space=pl.ANY)],
        out_specs=pl.BlockSpec(memory_space=pltpu.VMEM),
        scratch_shapes=[
            pltpu.VMEM((rows, width), jnp.bfloat16),
            pltpu.VMEM((rows, width), jnp.bfloat16),
            pltpu.VMEM((width, rows), jnp.bfloat16),
            pltpu.VMEM((2, rows, width), jnp.bfloat16),
            pltpu.VMEM((8, rows), jnp.float32),
            pltpu.VMEM((2, slabs, LANES), jnp.float32),
            pltpu.VMEM((2, slabs, LANES), jnp.float32),
            pltpu.VMEM((1, LANES), jnp.float32),
            pltpu.VMEM((n // 2, 1, LANES), jnp.float32),
            pltpu.SemaphoreType.DMA((chunks,)),
            pltpu.SemaphoreType.DMA((2, chunks)),
            pltpu.SemaphoreType.DMA((2, chunks)),
            pltpu.SemaphoreType.DMA((2,)),
            pltpu.SemaphoreType.DMA((2,)),
            pltpu.SemaphoreType.DMA((2,)),
            pltpu.SemaphoreType.DMA,
            pltpu.SemaphoreType.REGULAR((n.bit_length() - 1,)),
            pltpu.SemaphoreType.REGULAR,
            pltpu.VMEM((slabs, LANES), jnp.float32),
            pltpu.VMEM((slabs, LANES), jnp.float32),
            pltpu.VMEM((slabs, LANES), jnp.float32),
            pltpu.VMEM((slabs, LANES), jnp.float32),
            pltpu.SemaphoreType.DMA((2,)),
            pltpu.SemaphoreType.DMA((2,)),
        ],
        compiler_params=pltpu.CompilerParams(
            collective_id=0, has_side_effects=True, vmem_limit_bytes=63 * 2**20
        ),
        cost_estimate=pl.CostEstimate(
            flops=2 * tiles * rows * rows * width,
            bytes_accessed=2 * rows * width,
            transcendentals=tiles * rows * rows,
        ),
        name="pair_sums",
    )(embeddings)
    return out.reshape(rows)


def solution(mesh):
    return jax.shard_map(
        shards,
        mesh=mesh,
        in_specs=(P("dev", None),),
        out_specs=P("dev"),
        check_vma=False,
    )
```

```python
import functools
import math

import jax
import jax.numpy as jnp
from jax import lax
from jax.experimental import pallas as pl
from jax.experimental.pallas import tpu as pltpu
from jax.sharding import PartitionSpec as P

ROUNDS = 4
LANES = 128
CHUNK = 128
PART = 256
sharpness = 10.0


def bit_of(me, stride):
    return (me // stride) % 2


def flipped(me, stride):
    return me + stride * (1 - 2 * bit_of(me, stride))


def partners(n, me):
    top = n // 2
    found = []
    for first, second, extra in ((top, top // 2, 0), (top // 4, top // 8, 1)):
        parity = bit_of(me, first) + bit_of(me, second)
        if extra:
            parity = parity + me % 2
        parity = parity % 2
        a, b = flipped(me, first), flipped(me, second)
        target = a + parity * (b - a)
        source = b + parity * (a - b)
        found.append((target, source))
    return found


def normalize(values):
    widened = values.astype(jnp.float32)
    scaled = (
        widened
        * lax.rsqrt(jnp.mean(widened * widened, axis=1, keepdims=True) + 1e-06)
        / math.sqrt(values.shape[1])
    )
    return scaled.astype(jnp.bfloat16)


def kernel(
    n,
    emb_ref,
    out_ref,
    raw,
    normed,
    turned,
    held,
    acc,
    sums,
    back,
    part,
    parts,
    load_sem,
    send_sem,
    recv_sem,
    sums_send,
    sums_recv,
    part_send,
    part_recv,
    known,
    go,
    base,
    other,
    given,
    weights,
    base_sem,
    given_sem,
):
    rows = normed.shape[0]
    chunks = rows // CHUNK
    me = lax.axis_index("dev")

    def piece(c):
        return pl.ds(pl.multiple_of(c * CHUNK, CHUNK), CHUNK)

    def load(c):
        return pltpu.make_async_copy(
            emb_ref.at[piece(c)], raw.at[piece(c)], load_sem.at[c]
        )

    levels = n.bit_length() - 1
    flips = [flipped(me, 1 << level) - me for level in range(levels)]

    def across(mask):
        return me + sum(flips[level] for level in range(levels) if mask >> level & 1)

    barrier = pltpu.get_barrier_semaphore()
    for level in range(levels):
        pl.semaphore_signal(
            barrier,
            inc=1,
            device_id=(across(1 << level),),
            device_id_type=pl.DeviceIdType.MESH,
        )
    for c in range(chunks):
        load(c).start()

    routes = partners(n, me)
    early = (bit_of(me, n // 2) + bit_of(me, n // 4) + me % 2) % 2
    turns = (n // 2, n // 4, 1)
    acc[...] = jnp.zeros_like(acc)

    def block_copy(way, c):
        return pltpu.make_async_remote_copy(
            src_ref=normed.at[piece(c)],
            dst_ref=held.at[way, piece(c)],
            send_sem=send_sem.at[way, c],
            recv_sem=recv_sem.at[way, c],
            device_id=(routes[way][0],),
            device_id_type=pl.DeviceIdType.MESH,
        )

    def sums_copy(way):
        return pltpu.make_async_remote_copy(
            src_ref=sums.at[way],
            dst_ref=back.at[way],
            send_sem=sums_send.at[way],
            recv_sem=sums_recv.at[way],
            device_id=(routes[way][1],),
            device_id_type=pl.DeviceIdType.MESH,
        )

    def prepare(c):
        load(c).wait()
        normed[piece(c), :] = normalize(raw[piece(c), :])

    def turn(c):
        turned[:, piece(c)] = normed[piece(c), :].T

    prepare(0)
    pl.semaphore_wait(barrier, levels)
    for c in range(chunks):
        if c:
            prepare(c)

        @pl.when(early == 1)
        def _():
            block_copy(0, c).start()

        block_copy(1, c).start()

    for c in range(chunks):
        turn(c)

    def tile(block, fold):
        folded = None
        for t in range(rows // PART):
            columns = slice(t * PART, (t + 1) * PART)
            similarity = jnp.dot(
                block, turned[:, columns], preferred_element_type=jnp.float32
            )
            values = jnp.exp(sharpness * (similarity - 1.0))
            acc[:, columns] += jnp.sum(
                values.reshape(CHUNK // 8, 8, PART), axis=0
            )
            if fold:
                for u in range(0, PART, LANES):
                    term = values[:, u : u + LANES]
                    folded = term if folded is None else folded + term
        return folded

    def meet(way, c):
        block_copy(way, c).wait_recv()
        folded = tile(held[way, piece(c), :], True)
        for u in range(CHUNK // LANES):
            turned_sums = folded[u * LANES : (u + 1) * LANES].T
            sums[way, pl.ds(c * (CHUNK // LANES) + u, 1), :] = jnp.sum(
                turned_sums, axis=0, keepdims=True
            )

    @pl.loop(0, chunks)
    def _(c):
        tile(normed[piece(c), :], False)

    for level in range(levels):
        pl.semaphore_signal(
            known.at[level],
            inc=1,
            device_id=(across(1 << level),),
            device_id_type=pl.DeviceIdType.MESH,
        )
        pl.semaphore_wait(known.at[level], 1)

    @pl.when(early == 1)
    def _():
        for c in range(chunks // 2):
            block_copy(0, c).wait_send()
        pl.semaphore_signal(
            go,
            inc=1,
            device_id=(across(1),),
            device_id_type=pl.DeviceIdType.MESH,
        )

    @pl.when(early == 0)
    def _():
        pl.semaphore_wait(go, 1)
        for c in range(chunks):
            block_copy(0, c).start()

        @pl.loop(0, chunks)
        def _(c):
            meet(0, c)

        sums_copy(0).start()

    @pl.loop(0, chunks)
    def _(c):
        meet(1, c)

    sums_copy(1).start()

    def own():
        return jnp.concatenate(
            [
                jnp.sum(acc[:, t * LANES : (t + 1) * LANES], axis=0, keepdims=True)
                for t in range(rows // LANES)
            ],
            axis=0,
        )

    def plain_copy(src, dst, pair, device):
        return pltpu.make_async_remote_copy(
            src_ref=src,
            dst_ref=dst,
            send_sem=pair.at[0],
            recv_sem=pair.at[1],
            device_id=(device,),
            device_id_type=pl.DeviceIdType.MESH,
        )

    base_copy = plain_copy(base, other, base_sem, routes[0][0])
    given_copy = plain_copy(given, weights, given_sem, routes[0][1])

    kinds = ([], [])
    for mask in range(n - 1, 0, -1):
        kinds[sum(1 for turn in turns if mask & turn) % 2].append(mask)
    same = len(kinds[0])

    @pl.when(early == 0)
    def _():
        sums_copy(1).wait_recv()
        base[...] = own() + back[1]
        base_copy.start()
        given_copy.wait_recv()
        pltpu.make_async_copy(parts, parts, part_recv).wait()
        base_copy.wait_send()
        sums_copy(0).wait_send()
        for c in range(chunks):
            block_copy(0, c).wait_send()

    @pl.when(early == 1)
    def _():
        @pl.loop(0, chunks)
        def _(c):
            meet(0, c)

        for way in range(2):
            sums_copy(way).wait_recv()
        base_copy.wait_recv()
        theirs = 1.0 / (other[...] + sums[0])
        mine = 1.0 / (own() + back[0] + back[1])
        given[...] = theirs
        weights[...] = mine
        part[...] = jnp.sum(theirs + mine, axis=0, keepdims=True)
        given_copy.start()
        for kind in (1, 0):
            for slot, mask in enumerate(kinds[kind]):
                pltpu.make_async_remote_copy(
                    src_ref=part,
                    dst_ref=parts.at[slot],
                    send_sem=part_send.at[kind],
                    recv_sem=part_recv,
                    device_id=(across(mask),),
                    device_id_type=pl.DeviceIdType.MESH,
                ).start()
        parts[same] = part[...]
        head = parts.at[pl.ds(0, same)]
        pltpu.make_async_copy(head, head, part_recv).wait()
        given_copy.wait_send()
        for c in range(chunks // 2, chunks):
            block_copy(0, c).wait_send()
        pltpu.make_async_copy(head, head, part_send.at[0]).wait()
        pltpu.make_async_copy(parts, parts, part_send.at[1]).wait()

    sums_copy(1).wait_send()
    for c in range(chunks):
        block_copy(1, c).wait_send()
    total = jnp.sum(jnp.sum(parts[...], axis=0), axis=1, keepdims=True)
    out_ref[...] = weights[...] * (n * rows) / total


def shards(embeddings):
    n = lax.axis_size("dev")
    rows, width = embeddings.shape
    chunks = rows // CHUNK
    slabs = rows // LANES
    tiles = ROUNDS // 2 + 1
    out = pl.pallas_call(
        functools.partial(kernel, n),
        out_shape=jax.ShapeDtypeStruct((slabs, LANES), jnp.float32),
        in_specs=[pl.BlockSpec(memory_space=pl.ANY)],
        out_specs=pl.BlockSpec(memory_space=pltpu.VMEM),
        scratch_shapes=[
            pltpu.VMEM((rows, width), jnp.bfloat16),
            pltpu.VMEM((rows, width), jnp.bfloat16),
            pltpu.VMEM((width, rows), jnp.bfloat16),
            pltpu.VMEM((2, rows, width), jnp.bfloat16),
            pltpu.VMEM((8, rows), jnp.float32),
            pltpu.VMEM((2, slabs, LANES), jnp.float32),
            pltpu.VMEM((2, slabs, LANES), jnp.float32),
            pltpu.VMEM((1, LANES), jnp.float32),
            pltpu.VMEM((n // 2, 1, LANES), jnp.float32),
            pltpu.SemaphoreType.DMA((chunks,)),
            pltpu.SemaphoreType.DMA((2, chunks)),
            pltpu.SemaphoreType.DMA((2, chunks)),
            pltpu.SemaphoreType.DMA((2,)),
            pltpu.SemaphoreType.DMA((2,)),
            pltpu.SemaphoreType.DMA((2,)),
            pltpu.SemaphoreType.DMA,
            pltpu.SemaphoreType.REGULAR((n.bit_length() - 1,)),
            pltpu.SemaphoreType.REGULAR,
            pltpu.VMEM((slabs, LANES), jnp.float32),
            pltpu.VMEM((slabs, LANES), jnp.float32),
            pltpu.VMEM((slabs, LANES), jnp.float32),
            pltpu.VMEM((slabs, LANES), jnp.float32),
            pltpu.SemaphoreType.DMA((2,)),
            pltpu.SemaphoreType.DMA((2,)),
        ],
        compiler_params=pltpu.CompilerParams(
            collective_id=0, has_side_effects=True, vmem_limit_bytes=63 * 2**20
        ),
        cost_estimate=pl.CostEstimate(
            flops=2 * tiles * rows * rows * width,
            bytes_accessed=2 * rows * width,
            transcendentals=tiles * rows * rows,
        ),
        name="pair_sums",
    )(embeddings)
    return out.reshape(rows)


def solution(mesh):
    return jax.shard_map(
        shards,
        mesh=mesh,
        in_specs=(P("dev", None),),
        out_specs=P("dev"),
        check_vma=False,
    )
```

```python
import functools
import math

import jax
import jax.numpy as jnp
from jax import lax
from jax.experimental import pallas as pl
from jax.experimental.pallas import tpu as pltpu
from jax.sharding import PartitionSpec as P

ROUNDS = 4
LANES = 128
CHUNK = 256
sharpness = 10.0


def bit_of(me, stride):
    return (me // stride) % 2


def flipped(me, stride):
    return me + stride * (1 - 2 * bit_of(me, stride))


def partners(n, me):
    top = n // 2
    found = []
    for first, second, extra in ((top, top // 2, 0), (top // 4, top // 8, 1)):
        parity = bit_of(me, first) + bit_of(me, second)
        if extra:
            parity = parity + me % 2
        parity = parity % 2
        a, b = flipped(me, first), flipped(me, second)
        target = a + parity * (b - a)
        source = b + parity * (a - b)
        found.append((target, source))
    return found


def normalize(values):
    widened = values.astype(jnp.float32)
    scaled = (
        widened
        * lax.rsqrt(jnp.mean(widened * widened, axis=1, keepdims=True) + 1e-06)
        / math.sqrt(values.shape[1])
    )
    return scaled.astype(jnp.bfloat16)


def kernel(
    n,
    emb_ref,
    out_ref,
    raw,
    normed,
    turned,
    held,
    acc,
    sums,
    back,
    part,
    parts,
    load_sem,
    send_sem,
    recv_sem,
    sums_send,
    sums_recv,
    part_send,
    part_recv,
    known,
    go,
    base,
    other,
    given,
    weights,
    base_sem,
    given_sem,
):
    rows = normed.shape[0]
    chunks = rows // CHUNK
    me = lax.axis_index("dev")

    def piece(c):
        return pl.ds(pl.multiple_of(c * CHUNK, CHUNK), CHUNK)

    def load(c):
        return pltpu.make_async_copy(
            emb_ref.at[piece(c)], raw.at[piece(c)], load_sem.at[c]
        )

    levels = n.bit_length() - 1
    flips = [flipped(me, 1 << level) - me for level in range(levels)]

    def across(mask):
        return me + sum(flips[level] for level in range(levels) if mask >> level & 1)

    barrier = pltpu.get_barrier_semaphore()
    for level in range(levels):
        pl.semaphore_signal(
            barrier,
            inc=1,
            device_id=(across(1 << level),),
            device_id_type=pl.DeviceIdType.MESH,
        )
    for c in range(chunks):
        load(c).start()

    routes = partners(n, me)
    early = (bit_of(me, n // 2) + bit_of(me, n // 4) + me % 2) % 2
    turns = (n // 2, n // 4, 1)
    acc[...] = jnp.zeros_like(acc)

    def block_copy(way, c):
        return pltpu.make_async_remote_copy(
            src_ref=normed.at[piece(c)],
            dst_ref=held.at[way, piece(c)],
            send_sem=send_sem.at[way, c],
            recv_sem=recv_sem.at[way, c],
            device_id=(routes[way][0],),
            device_id_type=pl.DeviceIdType.MESH,
        )

    def sums_copy(way):
        return pltpu.make_async_remote_copy(
            src_ref=sums.at[way],
            dst_ref=back.at[way],
            send_sem=sums_send.at[way],
            recv_sem=sums_recv.at[way],
            device_id=(routes[way][1],),
            device_id_type=pl.DeviceIdType.MESH,
        )

    def prepare(c):
        load(c).wait()
        normed[piece(c), :] = normalize(raw[piece(c), :])

    def turn(c):
        turned[:, piece(c)] = normed[piece(c), :].T

    prepare(0)
    pl.semaphore_wait(barrier, levels)
    for c in range(chunks):
        if c:
            prepare(c)

        @pl.when(early == 1)
        def _():
            block_copy(0, c).start()

        block_copy(1, c).start()

    for c in range(chunks):
        turn(c)

    def tile(block, fold):
        folded = None
        for t in range(chunks):
            columns = slice(t * CHUNK, (t + 1) * CHUNK)
            similarity = jnp.dot(
                block, turned[:, columns], preferred_element_type=jnp.float32
            )
            values = jnp.exp(sharpness * (similarity - 1.0))
            acc[:, columns] += jnp.sum(
                values.reshape(CHUNK // 8, 8, CHUNK), axis=0
            )
            if fold:
                for u in range(0, CHUNK, LANES):
                    term = values[:, u : u + LANES]
                    folded = term if folded is None else folded + term
        return folded

    def meet(way, c):
        block_copy(way, c).wait_recv()
        folded = tile(held[way, piece(c), :], True)
        for u in range(CHUNK // LANES):
            turned_sums = folded[u * LANES : (u + 1) * LANES].T
            sums[way, pl.ds(c * (CHUNK // LANES) + u, 1), :] = jnp.sum(
                turned_sums, axis=0, keepdims=True
            )

    @pl.loop(0, chunks)
    def _(c):
        tile(normed[piece(c), :], False)

    for level in range(levels):
        pl.semaphore_signal(
            known.at[level],
            inc=1,
            device_id=(across(1 << level),),
            device_id_type=pl.DeviceIdType.MESH,
        )
        pl.semaphore_wait(known.at[level], 1)

    @pl.when(early == 1)
    def _():
        for c in range(chunks - 1):
            block_copy(0, c).wait_send()
        pl.semaphore_signal(
            go,
            inc=1,
            device_id=(across(1),),
            device_id_type=pl.DeviceIdType.MESH,
        )

    @pl.when(early == 0)
    def _():
        pl.semaphore_wait(go, 1)
        for c in range(chunks):
            block_copy(0, c).start()

        @pl.loop(0, chunks)
        def _(c):
            meet(0, c)

        sums_copy(0).start()

    @pl.loop(0, chunks)
    def _(c):
        meet(1, c)

    sums_copy(1).start()

    def own():
        return jnp.concatenate(
            [
                jnp.sum(acc[:, t * LANES : (t + 1) * LANES], axis=0, keepdims=True)
                for t in range(rows // LANES)
            ],
            axis=0,
        )

    def plain_copy(src, dst, pair, device):
        return pltpu.make_async_remote_copy(
            src_ref=src,
            dst_ref=dst,
            send_sem=pair.at[0],
            recv_sem=pair.at[1],
            device_id=(device,),
            device_id_type=pl.DeviceIdType.MESH,
        )

    base_copy = plain_copy(base, other, base_sem, routes[0][0])
    given_copy = plain_copy(given, weights, given_sem, routes[0][1])

    kinds = ([], [])
    for mask in range(n - 1, 0, -1):
        kinds[sum(1 for turn in turns if mask & turn) % 2].append(mask)
    same = len(kinds[0])

    @pl.when(early == 0)
    def _():
        sums_copy(1).wait_recv()
        base[...] = own() + back[1]
        base_copy.start()
        given_copy.wait_recv()
        pltpu.make_async_copy(parts, parts, part_recv).wait()
        base_copy.wait_send()
        sums_copy(0).wait_send()
        for c in range(chunks):
            block_copy(0, c).wait_send()

    @pl.when(early == 1)
    def _():
        @pl.loop(0, chunks)
        def _(c):
            meet(0, c)

        for way in range(2):
            sums_copy(way).wait_recv()
        base_copy.wait_recv()
        theirs = 1.0 / (other[...] + sums[0])
        mine = 1.0 / (own() + back[0] + back[1])
        given[...] = theirs
        weights[...] = mine
        part[...] = jnp.sum(theirs + mine, axis=0, keepdims=True)
        given_copy.start()
        for kind in (1, 0):
            for slot, mask in enumerate(kinds[kind]):
                pltpu.make_async_remote_copy(
                    src_ref=part,
                    dst_ref=parts.at[slot],
                    send_sem=part_send.at[kind],
                    recv_sem=part_recv,
                    device_id=(across(mask),),
                    device_id_type=pl.DeviceIdType.MESH,
                ).start()
        parts[same] = part[...]
        head = parts.at[pl.ds(0, same)]
        pltpu.make_async_copy(head, head, part_recv).wait()
        given_copy.wait_send()
        for c in range(chunks - 1, chunks):
            block_copy(0, c).wait_send()
        pltpu.make_async_copy(head, head, part_send.at[0]).wait()
        pltpu.make_async_copy(parts, parts, part_send.at[1]).wait()

    sums_copy(1).wait_send()
    for c in range(chunks):
        block_copy(1, c).wait_send()
    total = jnp.sum(jnp.sum(parts[...], axis=0), axis=1, keepdims=True)
    out_ref[...] = weights[...] * (n * rows) / total


def shards(embeddings):
    n = lax.axis_size("dev")
    rows, width = embeddings.shape
    chunks = rows // CHUNK
    slabs = rows // LANES
    tiles = ROUNDS // 2 + 1
    out = pl.pallas_call(
        functools.partial(kernel, n),
        out_shape=jax.ShapeDtypeStruct((slabs, LANES), jnp.float32),
        in_specs=[pl.BlockSpec(memory_space=pl.ANY)],
        out_specs=pl.BlockSpec(memory_space=pltpu.VMEM),
        scratch_shapes=[
            pltpu.VMEM((rows, width), jnp.bfloat16),
            pltpu.VMEM((rows, width), jnp.bfloat16),
            pltpu.VMEM((width, rows), jnp.bfloat16),
            pltpu.VMEM((2, rows, width), jnp.bfloat16),
            pltpu.VMEM((8, rows), jnp.float32),
            pltpu.VMEM((2, slabs, LANES), jnp.float32),
            pltpu.VMEM((2, slabs, LANES), jnp.float32),
            pltpu.VMEM((1, LANES), jnp.float32),
            pltpu.VMEM((n // 2, 1, LANES), jnp.float32),
            pltpu.SemaphoreType.DMA((chunks,)),
            pltpu.SemaphoreType.DMA((2, chunks)),
            pltpu.SemaphoreType.DMA((2, chunks)),
            pltpu.SemaphoreType.DMA((2,)),
            pltpu.SemaphoreType.DMA((2,)),
            pltpu.SemaphoreType.DMA((2,)),
            pltpu.SemaphoreType.DMA,
            pltpu.SemaphoreType.REGULAR((n.bit_length() - 1,)),
            pltpu.SemaphoreType.REGULAR,
            pltpu.VMEM((slabs, LANES), jnp.float32),
            pltpu.VMEM((slabs, LANES), jnp.float32),
            pltpu.VMEM((slabs, LANES), jnp.float32),
            pltpu.VMEM((slabs, LANES), jnp.float32),
            pltpu.SemaphoreType.DMA((2,)),
            pltpu.SemaphoreType.DMA((2,)),
        ],
        compiler_params=pltpu.CompilerParams(
            collective_id=0, has_side_effects=True, vmem_limit_bytes=63 * 2**20
        ),
        cost_estimate=pl.CostEstimate(
            flops=2 * tiles * rows * rows * width,
            bytes_accessed=2 * rows * width,
            transcendentals=tiles * rows * rows,
        ),
        name="pair_sums",
    )(embeddings)
    return out.reshape(rows)


def solution(mesh):
    return jax.shard_map(
        shards,
        mesh=mesh,
        in_specs=(P("dev", None),),
        out_specs=P("dev"),
        check_vma=False,
    )
```
